32 devices in a mesh: src: 4 (over y, x), rcv: 4 (over z), freq: 2 (over core).
Axes of the slice: x: 2, y: 2, z: 4, core: 2. Of those that a mesh axis runs over, the one named last changes fastest.
Arguments:
- wavefield: float32 [2, 2, 512, 512], P(None, 'freq', 'src', 'rcv'), may hold values from -6 to 6
- op_table: float32 [2, 64, 19], replicated, may hold values from -1.2 to 1.2
- vel_index: int32 [32], replicated, may hold values from 0 to 15
- interp_index: int32 [16, 2], replicated, may hold values from 0 to 62
- interp_weight: float32 [16, 2], replicated, may hold values from 0 to 1
- freq_perm: int32 [2], P('freq'), may hold values from 0 to 1, each once
Outputs:
- sunk: float32 [2, 2, 512, 512], P(None, 'freq', 'src', 'rcv')
- image: float32 [512], P('rcv')
The draws below stay inside these ranges and needn't reach their ends.
Inputs may be any that keep to these rules, and one draw needn't show every extreme that they name: `freq_perm`: each of the 2 frequencies is held by exactly one slot.
All inputs are finite; a program needn't handle non-finite values.
Results may differ from the reference program's by a relative error of at most 0.00012.
Values sent between devices are 32-bit elements; how exact they have to be, the bound alone decides.
No kernel may reach another device: no remote copies, remote signals or barrier semaphores. Data moves between devices by JAX's collectives and lax.ppermute only.
A program may use at most 64 MiB of HBM per device.

```python
import jax
import jax.numpy as jnp
from jax import lax

TAPS = 19
SUBSTEPS = 4
TILE = 16
NVEL = 16
NTAB = 64
RCV_DEV = 128
LX = 512
NF = 2
NTILE = 32
N_RCV = 4


def place_ends(entries, stream_key, low, top_value):
    spot = [jax.random.randint(jax.random.fold_in(stream_key, axis), (), 0, length) for axis, length in enumerate(entries.shape)]
    longest = entries.shape.index(max(entries.shape))
    beside = spot[:longest] + [(spot[longest] + 1) % entries.shape[longest]] + spot[longest + 1:]
    return entries.at[tuple(spot)].set(low).at[tuple(beside)].set(top_value)


def steps_of(key, shape, split, least, high):
    def one(position, blocks):
        steps = jax.random.uniform(jax.random.fold_in(jax.random.fold_in(key, 6), position), (blocks,), jnp.float32, least / len(split), high / len(split))
        return jnp.repeat(jnp.exp(steps), shape[position] // blocks).reshape((-1,) + (1,) * (len(shape) - position - 1))

    level = one(*split[0])
    for cut in split[1:]:
        level = level * one(*cut)
    return level


def bell_draw(key, extent, scale, reach, split=(), kind=jnp.bfloat16):
    level = steps_of(key, extent, split, -0.22, 0.18) if split else 1.0
    entries = jax.random.normal(key, extent, jnp.float32) * scale * level
    return jnp.minimum(jnp.maximum(entries, -reach), reach).astype(kind)


def setup_inputs(seed: int = 0) -> dict:
    streams_of = jax.random.split(jax.random.key(seed), 7)
    wavefield = bell_draw(streams_of[0], (2, NF, LX, LX), 1.0, 6.0, ((1, 2), (2, 4), (3, 4)), jnp.float32)
    op_table = bell_draw(streams_of[1], (2, NTAB, TAPS), 0.2, 1.2, (), jnp.float32)
    vel_index = place_ends(jax.random.randint(streams_of[2], (NTILE,), 0, NVEL), jax.random.fold_in(streams_of[2], 1), 0, NVEL - 1).astype(jnp.int32)
    interp_index = place_ends(jax.random.randint(streams_of[3], (NVEL, NF), 0, NTAB - 1), jax.random.fold_in(streams_of[3], 1), 0, (NTAB - 1) - 1).astype(jnp.int32)
    interp_weight = jnp.clip(jax.random.uniform(streams_of[4], (NVEL, NF), jnp.float32, 0.0, 1.0), 0.0, 1.0)
    freq_perm = jax.random.permutation(streams_of[5], NF).astype(jnp.int32)
    return dict(wavefield=wavefield, op_table=op_table, vel_index=vel_index, interp_index=interp_index, interp_weight=interp_weight, freq_perm=freq_perm)


def convolve(padded, coef_slot, along_axis, span_width):
    real_acc = None
    imag_acc = None
    for tap_index in range(coef_slot.shape[1]):
        window = lax.slice_in_dim(padded, tap_index, tap_index + span_width, axis=along_axis)
        coef_real = coef_slot[0, tap_index]
        coef_imag = coef_slot[1, tap_index]
        if along_axis == 2:
            coef_real = coef_real[None, :]
            coef_imag = coef_imag[None, :]
        else:
            coef_real = coef_real[:, None]
            coef_imag = coef_imag[:, None]
        term_real = coef_real * window[0] - coef_imag * window[1]
        term_imag = coef_real * window[1] + coef_imag * window[0]
        if real_acc is None:
            real_acc, imag_acc = term_real, term_imag
        else:
            real_acc = real_acc + term_real
            imag_acc = imag_acc + term_imag
    return jnp.stack([real_acc, imag_acc])


def reference(wavefield, op_table, vel_index, interp_index, interp_weight, freq_perm):
    table_row = interp_index[:, freq_perm]
    weights = interp_weight[:, freq_perm]
    lower_taps = op_table[:, table_row]
    upper_taps = op_table[:, table_row + 1]
    mixed = lower_taps * (1.0 - weights)[None, :, :, None] + upper_taps * weights[None, :, :, None]
    mixed_taps = jnp.transpose(mixed, (0, 2, 3, 1))
    velocity = vel_index[jnp.arange(LX) // TILE]
    coefficients = mixed_taps[..., velocity]
    half_taps = TAPS // 2

    def one_frequency(slot, carry):
        sunk_all, image_acc = carry
        field = lax.dynamic_index_in_dim(wavefield, slot, axis=1, keepdims=False)
        coef_slot = lax.dynamic_index_in_dim(coefficients, slot, axis=1, keepdims=False)

        def receiver_block(block, current):
            piece = lax.dynamic_slice_in_dim(current, block * RCV_DEV, RCV_DEV, axis=1)
            for substep in range(SUBSTEPS):
                padded = jnp.pad(piece, ((0, 0), (0, 0), (half_taps, half_taps)))
                piece = convolve(padded, coef_slot, 2, LX)
            return lax.dynamic_update_slice_in_dim(current, piece, block * RCV_DEV, axis=1)

        def source_block(block, current):
            piece = lax.dynamic_slice_in_dim(current, block * RCV_DEV, RCV_DEV, axis=2)
            for substep in range(SUBSTEPS):
                padded = jnp.pad(piece, ((0, 0), (half_taps, half_taps), (0, 0)))
                piece = convolve(padded, coef_slot, 1, LX)
            return lax.dynamic_update_slice_in_dim(current, piece, block * RCV_DEV, axis=2)

        field = lax.fori_loop(0, N_RCV, receiver_block, field)
        field = lax.fori_loop(0, N_RCV, source_block, field)
        sunk_all = lax.dynamic_update_index_in_dim(sunk_all, field, slot, axis=1)
        image_acc = image_acc + jnp.diagonal(field[0])
        return (sunk_all, image_acc)

    start_sunk = jnp.zeros_like(wavefield)
    start_image = jnp.zeros((LX,), wavefield.dtype)
    sunk, image = lax.fori_loop(0, NF, one_frequency, (start_sunk, start_image))
    return sunk, image
```

```python
import functools

import jax
import jax.numpy as jnp
from jax import lax
from jax.experimental import pallas as pl
from jax.experimental.pallas import tpu as pltpu
from jax.sharding import PartitionSpec as P

SUBSTEPS = 4
TILE = 16
VMEM_LIMIT = 32 * 1024 * 1024
F32 = jnp.float32
BF16 = jnp.bfloat16


def halves(value):
    high = value.astype(BF16)
    low = (value - high.astype(F32)).astype(BF16)
    return high, low


def dot(left, right):
    return jnp.dot(left, right, preferred_element_type=F32)


def dot3(left, right):
    left_high, left_low = left
    right_high, right_low = right
    return dot(left_high, right_high) + (dot(left_high, right_low) + dot(left_low, right_high))


def square_product(left, right):
    rows, cols = left[0].shape[0], right[0].shape[1]
    stacked = halves(jnp.concatenate(left, axis=0))
    beside = halves(jnp.concatenate(right, axis=1))
    full = dot3(stacked, beside)
    real = full[:rows, :cols] - full[rows:, cols:]
    imag = full[:rows, cols:] + full[rows:, :cols]
    return real, imag


def build_operator(start, lateral, width, taps, vel_ref, index_ref, weight_ref, perm_ref, table, band):
    window = 2 * width
    count = window // TILE
    seam = count - count // 4
    tiles = vel_ref.shape[0]
    slot = perm_ref[0]
    for position in range(count):
        tile = start // TILE + position - (count if position >= seam else 0)
        inside = jnp.logical_and(tile >= 0, tile < tiles).astype(F32)
        velocity = vel_ref[jnp.clip(tile, 0, tiles - 1)]
        row = index_ref[velocity, slot]
        weight = weight_ref[velocity, slot]
        low_weight = (1.0 - weight) * inside
        high_weight = weight * inside
        shift = (position * TILE - taps // 2) % window
        for part in range(2):
            mixed = table[part, pl.ds(row, 1), :] * low_weight + table[part, pl.ds(row + 1, 1), :] * high_weight
            spread = jnp.broadcast_to(mixed, (TILE, mixed.shape[1]))
            slanted = pltpu.roll(spread, 0, 1, stride=1, stride_axis=0)
            wide = jnp.concatenate([slanted, jnp.zeros((TILE, window - slanted.shape[1]), F32)], axis=1)
            band[part, pl.ds(position * TILE, TILE), :] = pltpu.roll(wide, shift, 1)
    once = (band[0], band[1])
    twice = square_product(once, once)
    four = square_product((twice[0][:width], twice[1][:width]), twice)
    place = lax.broadcasted_iota(jnp.int32, (width, window), 1)
    cell = start + jnp.where(place < window - width // 2, place, place - window)
    inside = jnp.logical_and(cell >= 0, cell < lateral)
    return jnp.where(inside, four[0], 0.0), jnp.where(inside, four[1], 0.0)


def fill_table(table_ref, table):
    table[...] = jnp.zeros_like(table)
    table[:, :, : table_ref.shape[2]] = table_ref[...]


def rcv_operator_kernel(lateral, vel_ref, index_ref, weight_ref, perm_ref, table_ref, full_ref, high_ref, low_ref, table, band):
    width = full_ref.shape[1] // 2
    fill_table(table_ref, table)
    start = lax.axis_index("rcv") * width
    real, imag = build_operator(
        start, lateral, width, table_ref.shape[2], vel_ref, index_ref, weight_ref, perm_ref, table, band
    )
    turned = jnp.concatenate([real.T, imag.T], axis=1)
    full_ref[...] = turned
    high_ref[...], low_ref[...] = halves(turned)


def src_operator_kernel(lateral, vel_ref, index_ref, weight_ref, perm_ref, table_ref, high_ref, low_ref, table, band):
    chunks, width = high_ref.shape[0], high_ref.shape[2] // 2
    fill_table(table_ref, table)
    for chunk in range(chunks):
        start = (lax.axis_index("src") * chunks + chunk) * width
        real, imag = build_operator(
            start, lateral, width, table_ref.shape[2], vel_ref, index_ref, weight_ref, perm_ref, table, band
        )
        high_ref[chunk], low_ref[chunk] = halves(jnp.concatenate([real, imag], axis=0))


def receiver_kernel(rim, wave_ref, first_ref, second_ref, full_ref, high_ref, low_ref, sunk_ref, head_ref, tail_ref, image_ref):
    rows, width = wave_ref.shape[1], wave_ref.shape[2]
    half = width // 2
    odd = lax.axis_index("freq") % 2 == 1
    lane = lax.broadcasted_iota(jnp.int32, (rows // 2, width), 1)
    extended = []
    for part in range(2):
        first, second = first_ref[part], second_ref[part]
        before = jnp.where(odd, second, first)
        after = jnp.where(odd, first, second)
        top = jnp.where(lane < half, after, before)
        bottom = pltpu.roll(jnp.where(lane < half, before, after), half, 1)
        halo = jnp.concatenate([top, bottom], axis=0)
        extended.append(jnp.concatenate([wave_ref[part], halo], axis=1))
    full = dot3(halves(jnp.concatenate(extended, axis=0)), (high_ref[...], low_ref[...]))
    real = full[:rows, :width] - full[rows:, width:]
    imag = full[:rows, width:] + full[rows:, :width]
    sunk_ref[0] = real
    sunk_ref[1] = imag
    chunks = rows // width
    ahead = lax.axis_index("src") * chunks - lax.axis_index("rcv")
    line = lax.broadcasted_iota(jnp.int32, (width, 2 * width), 0)
    image = jnp.zeros((1, width), F32)
    for chunk in range(chunks):
        away = ahead + chunk
        beside = jnp.logical_or(
            jnp.logical_and(away == 1, line < half), jnp.logical_and(away == -1, line >= half)
        )
        weights = jnp.where(away == 0, full_ref[:width], jnp.where(beside, full_ref[width:], 0.0))
        piece = slice(chunk * width, (chunk + 1) * width)
        terms = weights[:, :width] * real[piece] - weights[:, width:] * imag[piece]
        image = image + jnp.sum(terms, axis=0, keepdims=True)
    image_ref[...] = image
    edge = head_ref.shape[1]
    head_ref[0] = real[:edge]
    head_ref[1] = imag[:edge]
    tail_ref[0] = real[rows - edge :]
    tail_ref[1] = imag[rows - edge :]
    head_ref[0, edge - 1 :, :] = image
    tail_ref[0, :1, :] = image


def source_kernel(field_ref, before_ref, after_ref, high_ref, low_ref, out_ref):
    rows, width = field_ref.shape[1], field_ref.shape[2]
    half = width // 2
    chunks = rows // width
    edge = before_ref.shape[1]
    gap = jnp.zeros((half - edge, width), F32)
    for chunk in range(chunks):
        low, high = chunk * width, (chunk + 1) * width
        extended = []
        for part in range(2):
            if chunk + 1 < chunks:
                after = field_ref[part, high : high + half]
            else:
                after = jnp.concatenate([after_ref[part], gap], axis=0)
            if chunk > 0:
                before = field_ref[part, low - half : low]
            else:
                before = jnp.concatenate([gap, before_ref[part]], axis=0)
            extended.append(jnp.concatenate([field_ref[part, low:high], after, before], axis=0))
        full = dot3((high_ref[chunk], low_ref[chunk]), halves(jnp.concatenate(extended, axis=1)))
        out_ref[0, low:high] = full[:width, :width] - full[width:, width:]
        out_ref[1, low:high] = full[:width, width:] + full[width:, :width]


def around(axis_sizes, sign):
    rcv, freq = axis_sizes
    pairs = []
    for at in range(rcv):
        for slot in range(freq):
            target = at + (sign if slot % 2 == 0 else -sign)
            to_slot = slot
            if not 0 <= target < rcv:
                target, to_slot = at, slot ^ 1
            pairs.append((at * freq + slot, target * freq + to_slot))
    return pairs


def body(wavefield, op_table, vel_index, interp_index, interp_weight, freq_perm):
    rows, width = wavefield.shape[2], wavefield.shape[3]
    n_src, n_rcv, n_freq = (lax.axis_size(axis) for axis in ("src", "rcv", "freq"))
    lateral = width * n_rcv
    taps = op_table.shape[2]
    rim = SUBSTEPS * (taps // 2)
    edge = -(-(rim + 1) // 8) * 8
    half = width // 2
    chunks = rows // width
    wave = wavefield.reshape(2, rows, width)

    vmem = pl.BlockSpec(memory_space=pltpu.VMEM)
    smem = pl.BlockSpec(memory_space=pltpu.SMEM)
    params = pltpu.CompilerParams(vmem_limit_bytes=VMEM_LIMIT)
    tables = (vel_index, interp_index, interp_weight, freq_perm, op_table)
    scratch = [
        pltpu.VMEM((2, op_table.shape[1], width), F32),
        pltpu.VMEM((2, 2 * width, 2 * width), F32),
    ]
    cost = pl.CostEstimate(flops=6 * 2**28, bytes_accessed=2**20, transcendentals=0)

    top, bottom = wave[:, : rows // 2], wave[:, rows // 2 :]
    lower = jnp.concatenate([top[:, :, :half], bottom[:, :, :half]], axis=2)
    upper = jnp.concatenate([bottom[:, :, half:], top[:, :, half:]], axis=2)
    odd = lax.axis_index("freq") % 2 == 1
    backward = jnp.where(odd, upper, lower)
    forward = jnp.where(odd, lower, upper)
    second = lax.ppermute(backward, ("rcv", "freq"), around((n_rcv, n_freq), -1))
    first = lax.ppermute(forward, ("rcv", "freq"), around((n_rcv, n_freq), 1))

    square = (2 * width, 2 * width)
    rcv_full, rcv_high, rcv_low = pl.pallas_call(
        functools.partial(rcv_operator_kernel, lateral),
        out_shape=[
            jax.ShapeDtypeStruct(square, F32),
            jax.ShapeDtypeStruct(square, BF16),
            jax.ShapeDtypeStruct(square, BF16),
        ],
        in_specs=[smem] * 4 + [vmem],
        out_specs=[vmem] * 3,
        scratch_shapes=scratch,
        compiler_params=params,
        cost_estimate=cost,
        name="rcv_operator",
    )(*tables)
    field, head, tail, image = pl.pallas_call(
        functools.partial(receiver_kernel, rim),
        out_shape=[
            jax.ShapeDtypeStruct((2, rows, width), F32),
            jax.ShapeDtypeStruct((2, edge, width), F32),
            jax.ShapeDtypeStruct((2, edge, width), F32),
            jax.ShapeDtypeStruct((1, width), F32),
        ],
        in_specs=[vmem] * 6,
        out_specs=[vmem] * 4,
        compiler_params=params,
        name="receivers",
    )(wave, first, second, rcv_full, rcv_high, rcv_low)

    def from_src(value, distance):
        return lax.ppermute(value, "src", [(i, (i + distance) % n_src) for i in range(n_src)])

    before = from_src(tail, 1)
    after = from_src(head, -1)
    if n_src >= 3:
        parts = [image, before[0, :1], after[0, edge - 1 :]]
        parts += [from_src(image, distance) for distance in range(2, n_src - 1)]
        image = functools.reduce(jnp.add, parts)
    else:
        image = lax.psum(image, "src")
    src_high, src_low = pl.pallas_call(
        functools.partial(src_operator_kernel, lateral),
        out_shape=[jax.ShapeDtypeStruct((chunks,) + square, BF16)] * 2,
        in_specs=[smem] * 4 + [vmem],
        out_specs=[vmem] * 2,
        scratch_shapes=scratch,
        compiler_params=params,
        cost_estimate=cost,
        name="src_operator",
    )(*tables)
    if n_freq == 2:
        image = image + lax.ppermute(image, "freq", [(0, 1), (1, 0)])
    else:
        image = lax.psum(image, "freq")
    sunk = pl.pallas_call(
        source_kernel,
        out_shape=jax.ShapeDtypeStruct((2, rows, width), F32),
        in_specs=[vmem] * 5,
        out_specs=vmem,
        compiler_params=params,
        name="sources",
    )(field, before, after, src_high, src_low)
    return sunk.reshape(wavefield.shape), image.reshape(width)


def solution(mesh):
    in_specs = (P(None, "freq", "src", "rcv"), P(), P(), P(), P(), P("freq"))
    out_specs = (P(None, "freq", "src", "rcv"), P("rcv"))
    return jax.shard_map(body, mesh=mesh, in_specs=in_specs, out_specs=out_specs, check_vma=False)
```

```python
import functools

import jax
import jax.numpy as jnp
from jax import lax
from jax.experimental import pallas as pl
from jax.experimental.pallas import tpu as pltpu
from jax.sharding import PartitionSpec as P

SUBSTEPS = 4
TILE = 16
VMEM_LIMIT = 32 * 1024 * 1024
F32 = jnp.float32
BF16 = jnp.bfloat16


def halves(value):
    high = value.astype(BF16)
    low = (value - high.astype(F32)).astype(BF16)
    return high, low


def dot(left, right):
    return jnp.dot(left, right, preferred_element_type=F32)


def dot3(left, right):
    left_high, left_low = left
    right_high, right_low = right
    return dot(left_high, right_high) + (dot(left_high, right_low) + dot(left_low, right_high))


def square_product(left, right):
    rows, cols = left[0].shape[0], right[0].shape[1]
    stacked = halves(jnp.concatenate(left, axis=0))
    beside = halves(jnp.concatenate(right, axis=1))
    full = dot3(stacked, beside)
    real = full[:rows, :cols] - full[rows:, cols:]
    imag = full[:rows, cols:] + full[rows:, :cols]
    return real, imag


def tile_taps(starts, window, vel_ref, index_ref, weight_ref, perm_ref, table_ref, table):
    count = window // TILE
    tiles, slots = vel_ref.shape[1], index_ref.shape[0]
    velocities, entries, taps = index_ref.shape[1], table_ref.shape[2], table_ref.shape[0]
    place = lax.broadcasted_iota(jnp.int32, (count, tiles), 0)
    place = place - jnp.where(place >= count - count // 4, count, 0)
    tile = jnp.concatenate([start // TILE + place for start in starts], axis=0)
    lane = lax.broadcasted_iota(jnp.int32, tile.shape, 1)
    velocity = jnp.sum(jnp.where(lane == tile, vel_ref[...].astype(F32), 0.0), axis=1, keepdims=True)
    inside = jnp.sum(jnp.where(lane == tile, 1.0, 0.0), axis=1, keepdims=True)
    chosen = lax.broadcasted_iota(jnp.int32, (slots, velocities), 0) == perm_ref[...]
    index = jnp.sum(jnp.where(chosen, index_ref[...].astype(F32), 0.0), axis=0, keepdims=True)
    weight = jnp.sum(jnp.where(chosen, weight_ref[...], 0.0), axis=0, keepdims=True)
    rows = tile.shape[0]
    hit = lax.broadcasted_iota(jnp.int32, (rows, velocities), 1).astype(F32) == velocity
    index = jnp.sum(jnp.where(hit, index, 0.0), axis=1, keepdims=True)
    weight = jnp.sum(jnp.where(hit, weight, 0.0), axis=1, keepdims=True)
    entry = lax.broadcasted_iota(jnp.int32, (rows, entries), 1).astype(F32)
    mix = jnp.where(entry == index, 1.0 - weight, 0.0) + jnp.where(entry == index + 1.0, weight, 0.0)
    mix = mix * inside
    table[...] = jnp.zeros_like(table)
    found = []
    for part in range(2):
        table[part, :taps, :] = table_ref[:, part, :]
        found.append(
            lax.dot_general(
                mix, table[part], (((1,), (1,)), ((), ())), precision=lax.Precision.HIGHEST, preferred_element_type=F32
            )
        )
    return found


def fill_band(found, first, taps, band):
    window = band.shape[1]
    for position in range(window // TILE):
        shift = (position * TILE - taps // 2) % window
        for part in range(2):
            row = found[part][first + position : first + position + 1]
            spread = jnp.broadcast_to(row, (TILE, row.shape[1]))
            slanted = pltpu.roll(spread, 0, 1, stride=1, stride_axis=0)
            wide = jnp.concatenate([slanted, jnp.zeros((TILE, window - slanted.shape[1]), F32)], axis=1)
            band[part, pl.ds(position * TILE, TILE), :] = pltpu.roll(wide, shift, 1)


def four_substeps(start, lateral, once):
    window = once[0].shape[0]
    width = window // 2
    twice = square_product(once, once)
    four = square_product((twice[0][:width], twice[1][:width]), twice)
    place = lax.broadcasted_iota(jnp.int32, (width, window), 1)
    cell = start + jnp.where(place < window - width // 2, place, place - window)
    inside = jnp.logical_and(cell >= 0, cell < lateral)
    return jnp.where(inside, four[0], 0.0), jnp.where(inside, four[1], 0.0)


def pack_kernel(wave_ref, one_ref, two_ref):
    rows, width = wave_ref.shape[1], wave_ref.shape[2]
    half = width // 2
    odd = lax.axis_index("freq") % 2 == 1
    lane = lax.broadcasted_iota(jnp.int32, (rows // 2, width), 1)
    own = jnp.logical_xor(lane < half, odd)
    for part in range(2):
        top = wave_ref[part, : rows // 2]
        bottom = pltpu.roll(wave_ref[part, rows // 2 :], half, 1)
        one_ref[part] = jnp.where(own, top, bottom)
        two_ref[part] = jnp.where(own, bottom, top)


def rcv_operator_kernel(
    lateral, vel_ref, index_ref, weight_ref, perm_ref, table_ref, full_ref, high_ref, low_ref, src_ref, table, band
):
    width = full_ref.shape[1] // 2
    taps, window = table_ref.shape[0], 2 * width
    chunks = src_ref.shape[0]
    starts = [lax.axis_index("rcv") * width]
    starts += [(lax.axis_index("src") * chunks + chunk) * width for chunk in range(chunks)]
    found = tile_taps(starts, window, vel_ref, index_ref, weight_ref, perm_ref, table_ref, table)
    fill_band(found, 0, taps, band)
    for chunk in range(chunks):
        fill_band(found, (chunk + 1) * window // TILE, taps, src_ref.at[chunk])
    real, imag = four_substeps(starts[0], lateral, (band[0], band[1]))
    turned = jnp.concatenate([real.T, imag.T], axis=1)
    full_ref[...] = turned
    high_ref[...], low_ref[...] = halves(turned)


def src_operator_kernel(lateral, band_ref, high_ref, low_ref):
    chunks, width = high_ref.shape[0], high_ref.shape[2] // 2
    for chunk in range(chunks):
        start = (lax.axis_index("src") * chunks + chunk) * width
        real, imag = four_substeps(start, lateral, (band_ref[chunk, 0], band_ref[chunk, 1]))
        high_ref[chunk], low_ref[chunk] = halves(jnp.concatenate([real, imag], axis=0))


def receiver_kernel(wave_ref, first_ref, second_ref, full_ref, high_ref, low_ref, sunk_ref, one_ref, two_ref, image_ref):
    rows, width = wave_ref.shape[1], wave_ref.shape[2]
    half = width // 2
    odd = lax.axis_index("freq") % 2 == 1
    lane = lax.broadcasted_iota(jnp.int32, (rows // 2, width), 1)
    extended = []
    for part in range(2):
        first, second = first_ref[part], second_ref[part]
        before = jnp.where(odd, first, second)
        after = jnp.where(odd, second, first)
        top = jnp.where(lane < half, after, before)
        bottom = pltpu.roll(jnp.where(lane < half, before, after), half, 1)
        halo = jnp.concatenate([top, bottom], axis=0)
        extended.append(jnp.concatenate([wave_ref[part], halo], axis=1))
    full = dot3(halves(jnp.concatenate(extended, axis=0)), (high_ref[...], low_ref[...]))
    real = full[:rows, :width] - full[rows:, width:]
    imag = full[:rows, width:] + full[rows:, :width]
    sunk_ref[0] = real
    sunk_ref[1] = imag
    chunks = rows // width
    ahead = lax.axis_index("src") * chunks - lax.axis_index("rcv")
    line = lax.broadcasted_iota(jnp.int32, (width, 2 * width), 0)
    image = jnp.zeros((1, width), F32)
    for chunk in range(chunks):
        away = ahead + chunk
        beside = jnp.logical_or(
            jnp.logical_and(away == 1, line < half), jnp.logical_and(away == -1, line >= half)
        )
        weights = jnp.where(away == 0, full_ref[:width], jnp.where(beside, full_ref[width:], 0.0))
        piece = slice(chunk * width, (chunk + 1) * width)
        terms = weights[:, :width] * real[piece] - weights[:, width:] * imag[piece]
        image = image + jnp.sum(terms, axis=0, keepdims=True)
    image_ref[...] = image
    edge = one_ref.shape[1]
    row = lax.broadcasted_iota(jnp.int32, (edge, width), 0)
    head = (jnp.where(row == edge - 1, image, real[:edge]), imag[:edge])
    tail = (jnp.where(row == 0, image, real[rows - edge :]), imag[rows - edge :])
    up = lax.axis_index("src") % 2 == 0
    for part in range(2):
        one_ref[part] = jnp.where(up, tail[part], head[part])
        two_ref[part] = jnp.where(up, head[part], tail[part])


def source_kernel(field_ref, one_ref, two_ref, high_ref, low_ref, out_ref):
    rows, width = field_ref.shape[1], field_ref.shape[2]
    half = width // 2
    chunks = rows // width
    edge = one_ref.shape[1]
    up = lax.axis_index("src") % 2 == 0
    gap = jnp.zeros((half - edge, width), F32)
    for chunk in range(chunks):
        low, high = chunk * width, (chunk + 1) * width
        extended = []
        for part in range(2):
            if chunk + 1 < chunks:
                after = field_ref[part, high : high + half]
            else:
                after = jnp.concatenate([jnp.where(up, one_ref[part], two_ref[part]), gap], axis=0)
            if chunk > 0:
                before = field_ref[part, low - half : low]
            else:
                before = jnp.concatenate([gap, jnp.where(up, two_ref[part], one_ref[part])], axis=0)
            extended.append(jnp.concatenate([field_ref[part, low:high], after, before], axis=0))
        full = dot3((high_ref[chunk], low_ref[chunk]), halves(jnp.concatenate(extended, axis=1)))
        out_ref[0, low:high] = full[:width, :width] - full[width:, width:]
        out_ref[1, low:high] = full[:width, width:] + full[width:, :width]


def around(rcv, freq, sign):
    pairs = []
    for at in range(rcv):
        for slot in range(freq):
            target = at + (sign if slot % 2 == 0 else -sign)
            to_slot = slot
            if not 0 <= target < rcv:
                target, to_slot = at, slot ^ 1
            pairs.append((at * freq + slot, target * freq + to_slot))
    return pairs


def body(wavefield, op_table, vel_index, interp_index, interp_weight, freq_perm):
    rows, width = wavefield.shape[2], wavefield.shape[3]
    n_src, n_rcv, n_freq = (lax.axis_size(axis) for axis in ("src", "rcv", "freq"))
    lateral = width * n_rcv
    rim = SUBSTEPS * (op_table.shape[2] // 2)
    edge = -(-(rim + 1) // 8) * 8
    half = width // 2
    chunks = rows // width
    wave = wavefield.reshape(2, rows, width)

    vmem = pl.BlockSpec(memory_space=pltpu.VMEM)
    anywhere = pl.BlockSpec(memory_space=pltpu.HBM)
    params = pltpu.CompilerParams(vmem_limit_bytes=VMEM_LIMIT)
    cost = pl.CostEstimate(flops=6 * 2**28, bytes_accessed=2**20, transcendentals=0)

    tables = [
        vel_index.reshape(1, -1),
        interp_index.T,
        interp_weight.T,
        freq_perm.reshape(1, 1),
        op_table.transpose(2, 0, 1),
    ]
    packed = jax.ShapeDtypeStruct((2, rows // 2, width), F32)
    first, second = pl.pallas_call(
        pack_kernel,
        out_shape=[packed, packed],
        in_specs=[pl.BlockSpec(wave.shape, lambda: (0, 0, 0))],
        out_specs=[vmem] * 2,
        compiler_params=params,
        name="pack",
    )(wave)
    first = lax.ppermute(first, ("rcv", "freq"), around(n_rcv, n_freq, -1))
    second = lax.ppermute(second, ("rcv", "freq"), around(n_rcv, n_freq, 1))

    square = (2 * width, 2 * width)
    rcv_full, rcv_high, rcv_low, src_band = pl.pallas_call(
        functools.partial(rcv_operator_kernel, lateral),
        out_shape=[
            jax.ShapeDtypeStruct(square, F32),
            jax.ShapeDtypeStruct(square, BF16),
            jax.ShapeDtypeStruct(square, BF16),
            jax.ShapeDtypeStruct((chunks, 2) + square, F32),
        ],
        in_specs=[pl.BlockSpec(a.shape, lambda n=len(a.shape): (0,) * n) for a in tables],
        out_specs=[vmem] * 4,
        scratch_shapes=[pltpu.VMEM((2, width, op_table.shape[1]), F32), pltpu.VMEM((2,) + square, F32)],
        compiler_params=params,
        cost_estimate=cost,
        name="rcv_operator",
    )(*tables)
    field, one, two, image = pl.pallas_call(
        receiver_kernel,
        out_shape=[
            jax.ShapeDtypeStruct((2, rows, width), F32),
            jax.ShapeDtypeStruct((2, edge, width), F32),
            jax.ShapeDtypeStruct((2, edge, width), F32),
            jax.ShapeDtypeStruct((1, width), F32),
        ],
        in_specs=[vmem] * 6,
        out_specs=[vmem] * 4,
        compiler_params=params,
        name="receivers",
    )(wave, first, second, rcv_full, rcv_high, rcv_low)

    two = lax.ppermute(two, "src", [(i, (i - 1 if i % 2 == 0 else i + 1) % n_src) for i in range(n_src)])
    one = lax.ppermute(one, "src", [(i, i + 1 if i % 2 == 0 else i - 1) for i in range(n_src)])
    if n_src == 4:
        far = lax.ppermute(image, "src", [(i, i ^ 2) for i in range(n_src)])
    src_high, src_low = pl.pallas_call(
        functools.partial(src_operator_kernel, lateral),
        out_shape=[jax.ShapeDtypeStruct((chunks,) + square, BF16)] * 2,
        in_specs=[vmem],
        out_specs=[vmem] * 2,
        compiler_params=params,
        cost_estimate=pl.CostEstimate(flops=2**20, bytes_accessed=2**10, transcendentals=0),
        name="src_operator",
    )(src_band)
    if n_src == 4:
        up = lax.axis_index("src") % 2 == 0
        from_one = jnp.where(up, one[0, edge - 1 :], one[0, :1])
        from_two = jnp.where(up, two[0, :1], two[0, edge - 1 :])
        image = (image + from_one) + (from_two + far)
    else:
        image = lax.psum(image, "src")
    image, src_high = lax.optimization_barrier((image, src_high))
    if n_freq == 2:
        image = image + lax.ppermute(image, "freq", [(0, 1), (1, 0)])
    else:
        image = lax.psum(image, "freq")
    sunk = pl.pallas_call(
        source_kernel,
        out_shape=jax.ShapeDtypeStruct((2, rows, width), F32),
        in_specs=[vmem] * 5,
        out_specs=vmem,
        compiler_params=params,
        name="sources",
    )(field, one, two, src_high, src_low)
    return sunk.reshape(wavefield.shape), image.reshape(width)


def solution(mesh):
    in_specs = (P(None, "freq", "src", "rcv"), P(), P(), P(), P(), P("freq"))
    out_specs = (P(None, "freq", "src", "rcv"), P("rcv"))
    return jax.shard_map(body, mesh=mesh, in_specs=in_specs, out_specs=out_specs, check_vma=False)
```

```python
import functools

import jax
import jax.numpy as jnp
from jax import lax
from jax.experimental import pallas as pl
from jax.experimental.pallas import tpu as pltpu
from jax.sharding import PartitionSpec as P

SUBSTEPS = 4
TILE = 16
VMEM_LIMIT = 32 * 1024 * 1024
F32 = jnp.float32
BF16 = jnp.bfloat16


def halves(value):
    high = value.astype(BF16)
    low = (value - high.astype(F32)).astype(BF16)
    return high, low


def dot(left, right):
    return jnp.dot(left, right, preferred_element_type=F32)


def dot3(left, right):
    left_high, left_low = left
    right_high, right_low = right
    return dot(left_high, right_high) + (dot(left_high, right_low) + dot(left_low, right_high))


def complex_product(left, right):
    first = dot3(halves(left[0]), halves(right[0]))
    second = dot3(halves(left[1]), halves(right[1]))
    third = dot3(halves(left[0] + left[1]), halves(right[0] + right[1]))
    return first - second, third - first - second


def tile_taps(lateral_tiles, starts, window, small_ref, table_ref, table):
    count = window // TILE
    slots = (small_ref.shape[0] - 2) // 2
    tiles = velocities = small_ref.shape[1]
    entries, taps = table_ref.shape[2], table_ref.shape[0]
    place = lax.broadcasted_iota(jnp.int32, (count, tiles), 0)
    place = place - jnp.where(place >= count - count // 4, count, 0)
    tile = jnp.concatenate([start // TILE + place for start in starts], axis=0)
    lane = lax.broadcasted_iota(jnp.int32, tile.shape, 1)
    velocity = jnp.sum(jnp.where(lane == tile, small_ref[:1], 0.0), axis=1, keepdims=True)
    inside = jnp.logical_and(tile[:, :1] >= 0, tile[:, :1] < lateral_tiles).astype(F32)
    chosen = lax.broadcasted_iota(jnp.int32, (slots, velocities), 0).astype(F32) == small_ref[1:2, :1]
    index = jnp.sum(jnp.where(chosen, small_ref[2 : 2 + slots], 0.0), axis=0, keepdims=True)
    weight = jnp.sum(jnp.where(chosen, small_ref[2 + slots :], 0.0), axis=0, keepdims=True)
    rows = tile.shape[0]
    hit = lax.broadcasted_iota(jnp.int32, (rows, velocities), 1).astype(F32) == velocity
    index = jnp.sum(jnp.where(hit, index, 0.0), axis=1, keepdims=True)
    weight = jnp.sum(jnp.where(hit, weight, 0.0), axis=1, keepdims=True)
    entry = lax.broadcasted_iota(jnp.int32, (rows, entries), 1).astype(F32)
    mix = jnp.where(entry == index, 1.0 - weight, 0.0) + jnp.where(entry == index + 1.0, weight, 0.0)
    mix = mix * inside
    table[...] = jnp.zeros_like(table)
    found = []
    for part in range(2):
        table[part, :taps, :] = table_ref[:, part, :]
        found.append(
            lax.dot_general(
                mix, table[part], (((1,), (1,)), ((), ())), precision=lax.Precision.HIGHEST, preferred_element_type=F32
            )
        )
    return found


def fill_band(found, first, taps, band):
    window = band.shape[1]
    for position in range(window // TILE):
        shift = (position * TILE - taps // 2) % window
        for part in range(2):
            row = found[part][first + position : first + position + 1]
            spread = jnp.broadcast_to(row, (TILE, row.shape[1]))
            slanted = pltpu.roll(spread, 0, 1, stride=1, stride_axis=0)
            wide = jnp.concatenate([slanted, jnp.zeros((TILE, window - slanted.shape[1]), F32)], axis=1)
            band[part, pl.ds(position * TILE, TILE), :] = pltpu.roll(wide, shift, 1)


def four_substeps(start, lateral, once):
    window = once[0].shape[0]
    width = window // 2
    twice = complex_product(once, once)
    four = complex_product((twice[0][:width], twice[1][:width]), twice)
    place = lax.broadcasted_iota(jnp.int32, (width, window), 1)
    cell = start + jnp.where(place < window - width // 2, place, place - window)
    inside = jnp.logical_and(cell >= 0, cell < lateral)
    return jnp.where(inside, four[0], 0.0), jnp.where(inside, four[1], 0.0)


def groups_of(rows, width, rim):
    count = width // rim
    step = -(-rows // (8 * count)) * 8
    return width // count, [(low, min(low + step, rows)) for low in range(0, rows, step)]


def pack_kernel(rim, wave_ref, one_ref, two_ref):
    rows, width = wave_ref.shape[1], wave_ref.shape[2]
    span, groups = groups_of(rows, width, rim)
    odd = lax.axis_index("freq") % 2 == 1
    lane = lax.broadcasted_iota(jnp.int32, one_ref.shape[1:], 1)
    for part in range(2):
        packed = []
        for sign in (1, -1):
            message = wave_ref[part, groups[0][0] : groups[0][1]]
            for index, (low, high) in enumerate(groups[1:], 1):
                count = high - low
                place = lane[:count] if sign == 1 else width - 1 - lane[:count]
                moved = pltpu.roll(wave_ref[part, low:high], sign * index * span % width, 1)
                top = jnp.where(place // span == index, moved, message[:count])
                message = top if count == message.shape[0] else jnp.concatenate([top, message[count:]], axis=0)
            packed.append(message)
        one_ref[part] = jnp.where(odd, packed[1], packed[0])
        two_ref[part] = jnp.where(odd, packed[0], packed[1])


def rcv_operator_kernel(
    lateral, small_ref, table_ref, full_ref, high_ref, low_ref, found_ref, table, band
):
    width = full_ref.shape[1] // 2
    taps, window = table_ref.shape[0], 2 * width
    chunks = found_ref.shape[1] * TILE // window - 1
    starts = [lax.axis_index("rcv") * width]
    starts += [(lax.axis_index("src") * chunks + chunk) * width for chunk in range(chunks)]
    found = tile_taps(lateral // TILE, starts, window, small_ref, table_ref, table)
    fill_band(found, 0, taps, band)
    for part in range(2):
        found_ref[part] = found[part]
    real, imag = four_substeps(starts[0], lateral, (band[0], band[1]))
    turned = jnp.concatenate([real.T, imag.T], axis=1)
    full_ref[...] = turned
    high_ref[...], low_ref[...] = halves(turned)


def src_operator_kernel(lateral, taps, found_ref, high_ref, low_ref, band):
    chunks, width = high_ref.shape[0], high_ref.shape[2] // 2
    found = (found_ref[0], found_ref[1])
    for chunk in range(chunks):
        start = (lax.axis_index("src") * chunks + chunk) * width
        fill_band(found, (chunk + 1) * 2 * width // TILE, taps, band)
        real, imag = four_substeps(start, lateral, (band[0], band[1]))
        high_ref[chunk], low_ref[chunk] = halves(jnp.concatenate([real, imag], axis=0))


def receiver_kernel(rim, wave_ref, first_ref, second_ref, full_ref, high_ref, low_ref, sunk_ref, one_ref, two_ref, image_ref):
    rows, width = sunk_ref.shape[1], sunk_ref.shape[2]
    half = width // 2
    span, groups = groups_of(rows, width, rim)
    odd = lax.axis_index("freq") % 2 == 1
    extended = []
    for part in range(2):
        halos = []
        first, second = first_ref[part], second_ref[part]
        before = jnp.where(odd, first, second)
        after = jnp.where(odd, second, first)
        for index, (low, high) in enumerate(groups):
            left, right = after[: high - low], before[: high - low]
            if index:
                left = pltpu.roll(left, -index * span % width, 1)
                right = pltpu.roll(right, index * span % width, 1)
            lane = lax.broadcasted_iota(jnp.int32, left.shape, 1)
            halos.append(jnp.where(lane < half, left, right))
        extended.append(jnp.concatenate([wave_ref[part], jnp.concatenate(halos, axis=0)], axis=1))
    full = dot3(halves(jnp.concatenate(extended, axis=0)), (high_ref[...], low_ref[...]))
    real = full[:rows, :width] - full[rows:, width:]
    imag = full[:rows, width:] + full[rows:, :width]
    sunk_ref[0] = real
    sunk_ref[1] = imag
    chunks = rows // width
    ahead = lax.axis_index("src") * chunks - lax.axis_index("rcv")
    line = lax.broadcasted_iota(jnp.int32, (width, 2 * width), 0)
    image = jnp.zeros((1, width), F32)
    for chunk in range(chunks):
        away = ahead + chunk
        beside = jnp.logical_or(
            jnp.logical_and(away == 1, line < half), jnp.logical_and(away == -1, line >= half)
        )
        weights = jnp.where(away == 0, full_ref[:width], jnp.where(beside, full_ref[width:], 0.0))
        piece = slice(chunk * width, (chunk + 1) * width)
        terms = weights[:, :width] * real[piece] - weights[:, width:] * imag[piece]
        image = image + jnp.sum(terms, axis=0, keepdims=True)
    image_ref[...] = image
    edge = one_ref.shape[1]
    row = lax.broadcasted_iota(jnp.int32, (edge, width), 0)
    head = (jnp.where(row == edge - 1, image, real[:edge]), imag[:edge])
    tail = (jnp.where(row == 0, image, real[rows - edge :]), imag[rows - edge :])
    up = lax.axis_index("src") % 2 == 0
    for part in range(2):
        one_ref[part] = jnp.where(up, tail[part], head[part])
        two_ref[part] = jnp.where(up, head[part], tail[part])


def source_kernel(field_ref, two_ref, one_ref, high_ref, low_ref, out_ref):
    rows, width = field_ref.shape[1], field_ref.shape[2]
    half = width // 2
    chunks = rows // width
    edge = one_ref.shape[1]
    up = lax.axis_index("src") % 2 == 0
    gap = jnp.zeros((half - edge, width), F32)
    for chunk in range(chunks):
        low, high = chunk * width, (chunk + 1) * width
        extended = []
        for part in range(2):
            if chunk + 1 < chunks:
                after = field_ref[part, high : high + half]
            else:
                after = jnp.concatenate([jnp.where(up, one_ref[part], two_ref[part]), gap], axis=0)
            if chunk > 0:
                before = field_ref[part, low - half : low]
            else:
                before = jnp.concatenate([gap, jnp.where(up, two_ref[part], one_ref[part])], axis=0)
            extended.append(jnp.concatenate([field_ref[part, low:high], after, before], axis=0))
        full = dot3((high_ref[chunk], low_ref[chunk]), halves(jnp.concatenate(extended, axis=1)))
        out_ref[0, low:high] = full[:width, :width] - full[width:, width:]
        out_ref[1, low:high] = full[:width, width:] + full[width:, :width]


def around(rcv, freq, sign):
    pairs = []
    for at in range(rcv):
        for slot in range(freq):
            target = at + (sign if slot % 2 == 0 else -sign)
            to_slot = slot
            if not 0 <= target < rcv:
                target, to_slot = at, slot ^ 1
            pairs.append((at * freq + slot, target * freq + to_slot))
    return pairs


def body(wavefield, op_table, vel_index, interp_index, interp_weight, freq_perm):
    rows, width = wavefield.shape[2], wavefield.shape[3]
    n_src, n_rcv, n_freq = (lax.axis_size(axis) for axis in ("src", "rcv", "freq"))
    lateral = width * n_rcv
    rim = SUBSTEPS * (op_table.shape[2] // 2)
    edge = -(-(rim + 1) // 8) * 8
    half = width // 2
    chunks = rows // width
    wave = wavefield.reshape(2, rows, width)

    vmem = pl.BlockSpec(memory_space=pltpu.VMEM)
    anywhere = pl.BlockSpec(memory_space=pltpu.HBM)
    params = pltpu.CompilerParams(vmem_limit_bytes=VMEM_LIMIT)
    cost = pl.CostEstimate(flops=6 * 2**28, bytes_accessed=2**20, transcendentals=0)

    small = max(vel_index.shape[0], interp_index.shape[0], width)
    rows_of = lambda a: jnp.pad(a.astype(F32), ((0, 0), (0, small - a.shape[1])))
    tables = [
        jnp.concatenate(
            [rows_of(vel_index.reshape(1, -1)), jnp.pad(freq_perm, (0, small - 1)).astype(F32).reshape(1, -1), rows_of(interp_index.T), rows_of(interp_weight.T)]
        ),
        op_table.transpose(2, 0, 1),
    ]
    _, groups = groups_of(rows, width, rim)
    packed = jax.ShapeDtypeStruct((2, groups[0][1], width), F32)
    first, second = pl.pallas_call(
        functools.partial(pack_kernel, rim),
        out_shape=[packed, packed],
        in_specs=[vmem],
        out_specs=[vmem] * 2,
        compiler_params=params,
        name="pack",
    )(wave)
    first = lax.ppermute(first, ("rcv", "freq"), around(n_rcv, n_freq, -1))
    second = lax.ppermute(second, ("rcv", "freq"), around(n_rcv, n_freq, 1))

    square = (2 * width, 2 * width)
    rcv_full, rcv_high, rcv_low, found = pl.pallas_call(
        functools.partial(rcv_operator_kernel, lateral),
        out_shape=[
            jax.ShapeDtypeStruct(square, F32),
            jax.ShapeDtypeStruct(square, BF16),
            jax.ShapeDtypeStruct(square, BF16),
            jax.ShapeDtypeStruct((2, (chunks + 1) * 2 * width // TILE, width), F32),
        ],
        in_specs=[vmem] * 2,
        out_specs=[vmem] * 4,
        scratch_shapes=[pltpu.VMEM((2, width, op_table.shape[1]), F32), pltpu.VMEM((2,) + square, F32)],
        compiler_params=params,
        cost_estimate=cost,
        name="rcv_operator",
    )(*tables)
    field, one, two, image = pl.pallas_call(
        functools.partial(receiver_kernel, rim),
        out_shape=[
            jax.ShapeDtypeStruct((2, rows, width), F32),
            jax.ShapeDtypeStruct((2, edge, width), F32),
            jax.ShapeDtypeStruct((2, edge, width), F32),
            jax.ShapeDtypeStruct((1, width), F32),
        ],
        in_specs=[vmem] * 6,
        out_specs=[vmem] * 4,
        compiler_params=params,
        name="receivers",
    )(wave, first, second, rcv_full, rcv_high, rcv_low)

    two = lax.ppermute(two, "src", [(i, (i - 1 if i % 2 == 0 else i + 1) % n_src) for i in range(n_src)])
    one = lax.ppermute(one, "src", [(i, i + 1 if i % 2 == 0 else i - 1) for i in range(n_src)])
    if n_src == 4:
        far = lax.ppermute(image, "src", [(i, i ^ 2) for i in range(n_src)])
    src_high, src_low = pl.pallas_call(
        functools.partial(src_operator_kernel, lateral, op_table.shape[2]),
        out_shape=[jax.ShapeDtypeStruct((chunks,) + square, BF16)] * 2,
        in_specs=[vmem],
        out_specs=[vmem] * 2,
        scratch_shapes=[pltpu.VMEM((2,) + square, F32)],
        compiler_params=params,
        cost_estimate=pl.CostEstimate(flops=2**20, bytes_accessed=2**10, transcendentals=0),
        name="src_operator",
    )(found)
    if n_src == 4:
        up = lax.axis_index("src") % 2 == 0
        from_one = jnp.where(up, one[0, edge - 1 :], one[0, :1])
        from_two = jnp.where(up, two[0, :1], two[0, edge - 1 :])
        image = (image + from_one) + (from_two + far)
    else:
        image = lax.psum(image, "src")
    image, src_high = lax.optimization_barrier((image, src_high))
    if n_freq == 2:
        image = image + lax.ppermute(image, "freq", [(0, 1), (1, 0)])
    else:
        image = lax.psum(image, "freq")
    sunk = pl.pallas_call(
        source_kernel,
        out_shape=jax.ShapeDtypeStruct((2, rows, width), F32),
        in_specs=[vmem] * 5,
        out_specs=vmem,
        compiler_params=params,
        name="sources",
    )(field, two, one, src_high, src_low)
    return sunk.reshape(wavefield.shape), image.reshape(width)


def solution(mesh):
    in_specs = (P(None, "freq", "src", "rcv"), P(), P(), P(), P(), P("freq"))
    out_specs = (P(None, "freq", "src", "rcv"), P("rcv"))
    return jax.shard_map(body, mesh=mesh, in_specs=in_specs, out_specs=out_specs, check_vma=False)
```

```python
import functools

import jax
import jax.numpy as jnp
from jax import lax
from jax.experimental import pallas as pl
from jax.experimental.pallas import tpu as pltpu
from jax.sharding import PartitionSpec as P

SUBSTEPS = 4
TILE = 16
VMEM_LIMIT = 32 * 1024 * 1024
F32 = jnp.float32
BF16 = jnp.bfloat16


def halves(value):
    high = value.astype(BF16)
    low = (value - high.astype(F32)).astype(BF16)
    return high, low


def dot(left, right):
    return jnp.dot(left, right, preferred_element_type=F32)


def dot3(left, right):
    left_high, left_low = left
    right_high, right_low = right
    return dot(left_high, right_high) + (dot(left_high, right_low) + dot(left_low, right_high))


def complex_product(left, right):
    first = dot3(halves(left[0]), halves(right[0]))
    second = dot3(halves(left[1]), halves(right[1]))
    third = dot3(halves(left[0] + left[1]), halves(right[0] + right[1]))
    return first - second, third - first - second


def tile_taps(lateral_tiles, starts, window, small_ref, table_ref, table):
    count = window // TILE
    slots = (small_ref.shape[0] - 2) // 2
    tiles = velocities = small_ref.shape[1]
    entries, taps = table_ref.shape[2], table_ref.shape[0]
    place = lax.broadcasted_iota(jnp.int32, (count, tiles), 0)
    place = place - jnp.where(place >= count - count // 4, count, 0)
    tile = jnp.concatenate([start // TILE + place for start in starts], axis=0)
    lane = lax.broadcasted_iota(jnp.int32, tile.shape, 1)
    velocity = jnp.sum(jnp.where(lane == tile, small_ref[:1], 0.0), axis=1, keepdims=True)
    inside = jnp.logical_and(tile[:, :1] >= 0, tile[:, :1] < lateral_tiles).astype(F32)
    chosen = lax.broadcasted_iota(jnp.int32, (slots, velocities), 0).astype(F32) == small_ref[1:2, :1]
    index = jnp.sum(jnp.where(chosen, small_ref[2 : 2 + slots], 0.0), axis=0, keepdims=True)
    weight = jnp.sum(jnp.where(chosen, small_ref[2 + slots :], 0.0), axis=0, keepdims=True)
    rows = tile.shape[0]
    hit = lax.broadcasted_iota(jnp.int32, (rows, velocities), 1).astype(F32) == velocity
    index = jnp.sum(jnp.where(hit, index, 0.0), axis=1, keepdims=True)
    weight = jnp.sum(jnp.where(hit, weight, 0.0), axis=1, keepdims=True)
    entry = lax.broadcasted_iota(jnp.int32, (rows, entries), 1).astype(F32)
    mix = jnp.where(entry == index, 1.0 - weight, 0.0) + jnp.where(entry == index + 1.0, weight, 0.0)
    mix = mix * inside
    table[...] = jnp.zeros_like(table)
    found = []
    for part in range(2):
        table[part, :taps, :] = table_ref[:, part, :]
        found.append(
            lax.dot_general(
                mix, table[part], (((1,), (1,)), ((), ())), precision=lax.Precision.HIGHEST, preferred_element_type=F32
            )
        )
    return found


def fill_band(found, first, taps, band):
    window = band.shape[1]
    for position in range(window // TILE):
        shift = (position * TILE - taps // 2) % window
        for part in range(2):
            row = found[part][first + position : first + position + 1]
            spread = jnp.broadcast_to(row, (TILE, row.shape[1]))
            slanted = pltpu.roll(spread, 0, 1, stride=1, stride_axis=0)
            wide = jnp.concatenate([slanted, jnp.zeros((TILE, window - slanted.shape[1]), F32)], axis=1)
            band[part, pl.ds(position * TILE, TILE), :] = pltpu.roll(wide, shift, 1)


def four_substeps(start, lateral, once):
    window = once[0].shape[0]
    width = window // 2
    twice = complex_product(once, once)
    four = complex_product((twice[0][:width], twice[1][:width]), twice)
    place = lax.broadcasted_iota(jnp.int32, (width, window), 1)
    cell = start + jnp.where(place < window - width // 2, place, place - window)
    inside = jnp.logical_and(cell >= 0, cell < lateral)
    return jnp.where(inside, four[0], 0.0), jnp.where(inside, four[1], 0.0)


def groups_of(rows, width, rim):
    count = width // rim
    step = -(-rows // (8 * count)) * 8
    return width // count, [(low, min(low + step, rows)) for low in range(0, rows, step)]


def pack_kernel(rim, wave_ref, one_ref, two_ref):
    rows, width = wave_ref.shape[1], wave_ref.shape[2]
    span, groups = groups_of(rows, width, rim)
    odd = lax.axis_index("freq") % 2 == 1
    lane = lax.broadcasted_iota(jnp.int32, one_ref.shape[1:], 1)
    for part in range(2):
        packed = []
        for sign in (1, -1):
            message = wave_ref[part, groups[0][0] : groups[0][1]]
            for index, (low, high) in enumerate(groups[1:], 1):
                count = high - low
                place = lane[:count] if sign == 1 else width - 1 - lane[:count]
                moved = pltpu.roll(wave_ref[part, low:high], sign * index * span % width, 1)
                top = jnp.where(place // span == index, moved, message[:count])
                message = top if count == message.shape[0] else jnp.concatenate([top, message[count:]], axis=0)
            packed.append(message)
        one_ref[part] = jnp.where(odd, packed[1], packed[0])
        two_ref[part] = jnp.where(odd, packed[0], packed[1])


def rcv_operator_kernel(
    lateral, small_ref, table_ref, full_ref, high_ref, low_ref, found_ref, table, band
):
    width = full_ref.shape[1] // 2
    taps, window = table_ref.shape[0], 2 * width
    chunks = found_ref.shape[1] * TILE // window - 1
    starts = [lax.axis_index("rcv") * width]
    starts += [(lax.axis_index("src") * chunks + chunk) * width for chunk in range(chunks)]
    found = tile_taps(lateral // TILE, starts, window, small_ref, table_ref, table)
    fill_band(found, 0, taps, band)
    for part in range(2):
        found_ref[part] = found[part]
    real, imag = four_substeps(starts[0], lateral, (band[0], band[1]))
    turned = jnp.concatenate([real.T, imag.T], axis=1)
    full_ref[...] = turned
    high_ref[...], low_ref[...] = halves(turned)


def src_operator_kernel(lateral, taps, found_ref, high_ref, low_ref, band):
    chunks, width = high_ref.shape[0], high_ref.shape[2] // 2
    found = (found_ref[0], found_ref[1])
    for chunk in range(chunks):
        start = (lax.axis_index("src") * chunks + chunk) * width
        fill_band(found, (chunk + 1) * 2 * width // TILE, taps, band)
        real, imag = four_substeps(start, lateral, (band[0], band[1]))
        high_ref[chunk], low_ref[chunk] = halves(jnp.concatenate([real, imag], axis=0))


def receiver_kernel(rim, wave_ref, first_ref, second_ref, full_ref, high_ref, low_ref, sunk_ref, one_ref, two_ref, image_ref):
    rows, width = sunk_ref.shape[1], sunk_ref.shape[2]
    half = width // 2
    span, groups = groups_of(rows, width, rim)
    odd = lax.axis_index("freq") % 2 == 1
    extended = []
    for part in range(2):
        halos = []
        first, second = first_ref[part], second_ref[part]
        before = jnp.where(odd, first, second)
        after = jnp.where(odd, second, first)
        for index, (low, high) in enumerate(groups):
            left, right = after[: high - low], before[: high - low]
            if index:
                left = pltpu.roll(left, -index * span % width, 1)
                right = pltpu.roll(right, index * span % width, 1)
            lane = lax.broadcasted_iota(jnp.int32, left.shape, 1)
            halos.append(jnp.where(lane < half, left, right))
        extended.append(jnp.concatenate([wave_ref[part], jnp.concatenate(halos, axis=0)], axis=1))
    full = dot3(halves(jnp.concatenate(extended, axis=0)), (high_ref[...], low_ref[...]))
    real = full[:rows, :width] - full[rows:, width:]
    imag = full[:rows, width:] + full[rows:, :width]
    sunk_ref[0] = real
    sunk_ref[1] = imag
    chunks = rows // width
    ahead = lax.axis_index("src") * chunks - lax.axis_index("rcv")
    line = lax.broadcasted_iota(jnp.int32, (width, 2 * width), 0)
    image = jnp.zeros((1, width), F32)
    for chunk in range(chunks):
        away = ahead + chunk
        beside = jnp.logical_or(
            jnp.logical_and(away == 1, line < half), jnp.logical_and(away == -1, line >= half)
        )
        weights = jnp.where(away == 0, full_ref[:width], jnp.where(beside, full_ref[width:], 0.0))
        piece = slice(chunk * width, (chunk + 1) * width)
        terms = weights[:, :width] * real[piece] - weights[:, width:] * imag[piece]
        image = image + jnp.sum(terms, axis=0, keepdims=True)
    image_ref[...] = image
    edge = one_ref.shape[1]
    row = lax.broadcasted_iota(jnp.int32, (edge, width), 0)
    head = (jnp.where(row == edge - 1, image, real[:edge]), imag[:edge])
    tail = (jnp.where(row == 0, image, real[rows - edge :]), imag[rows - edge :])
    up = lax.axis_index("src") % 2 == 0
    for part in range(2):
        one_ref[part] = jnp.where(up, tail[part], head[part])
        two_ref[part] = jnp.where(up, head[part], tail[part])


def source_kernel(field_ref, two_ref, one_ref, high_ref, low_ref, *rest):
    rows, width = field_ref.shape[1], field_ref.shape[2]
    half = width // 2
    chunks = rows // width
    edge = one_ref.shape[1]
    up = lax.axis_index("src") % 2 == 0
    *image_refs, out_ref, image_ref = rest
    image_ref[...] = functools.reduce(jnp.add, [ref[...] for ref in image_refs])
    gap = jnp.zeros((half - edge, width), F32)
    for chunk in range(chunks):
        low, high = chunk * width, (chunk + 1) * width
        extended = []
        for part in range(2):
            if chunk + 1 < chunks:
                after = field_ref[part, high : high + half]
            else:
                after = jnp.concatenate([jnp.where(up, one_ref[part], two_ref[part]), gap], axis=0)
            if chunk > 0:
                before = field_ref[part, low - half : low]
            else:
                before = jnp.concatenate([gap, jnp.where(up, two_ref[part], one_ref[part])], axis=0)
            extended.append(jnp.concatenate([field_ref[part, low:high], after, before], axis=0))
        full = dot3((high_ref[chunk], low_ref[chunk]), halves(jnp.concatenate(extended, axis=1)))
        out_ref[0, low:high] = full[:width, :width] - full[width:, width:]
        out_ref[1, low:high] = full[:width, width:] + full[width:, :width]


def around(rcv, freq, sign):
    pairs = []
    for at in range(rcv):
        for slot in range(freq):
            target = at + (sign if slot % 2 == 0 else -sign)
            to_slot = slot
            if not 0 <= target < rcv:
                target, to_slot = at, slot ^ 1
            pairs.append((at * freq + slot, target * freq + to_slot))
    return pairs


def between(src, freq):
    pairs = []
    for at in range(src):
        target = at - 1 if at % 2 == 0 else at + 1
        for slot in range(freq):
            ends = not 0 <= target < src
            pairs.append((at * freq + slot, at * freq + (slot ^ 1) if ends else target * freq + slot))
    return pairs


def body(wavefield, op_table, vel_index, interp_index, interp_weight, freq_perm):
    rows, width = wavefield.shape[2], wavefield.shape[3]
    n_src, n_rcv, n_freq = (lax.axis_size(axis) for axis in ("src", "rcv", "freq"))
    lateral = width * n_rcv
    rim = SUBSTEPS * (op_table.shape[2] // 2)
    edge = -(-(rim + 1) // 8) * 8
    half = width // 2
    chunks = rows // width
    wave = wavefield.reshape(2, rows, width)

    vmem = pl.BlockSpec(memory_space=pltpu.VMEM)
    anywhere = pl.BlockSpec(memory_space=pltpu.HBM)
    params = pltpu.CompilerParams(vmem_limit_bytes=VMEM_LIMIT)
    cost = pl.CostEstimate(flops=6 * 2**28, bytes_accessed=2**20, transcendentals=0)

    small = max(vel_index.shape[0], interp_index.shape[0], width)
    rows_of = lambda a: jnp.pad(a.astype(F32), ((0, 0), (0, small - a.shape[1])))
    tables = [
        jnp.concatenate(
            [rows_of(vel_index.reshape(1, -1)), jnp.pad(freq_perm, (0, small - 1)).astype(F32).reshape(1, -1), rows_of(interp_index.T), rows_of(interp_weight.T)]
        ),
        op_table.transpose(2, 0, 1),
    ]
    _, groups = groups_of(rows, width, rim)
    packed = jax.ShapeDtypeStruct((2, groups[0][1], width), F32)
    first, second = pl.pallas_call(
        functools.partial(pack_kernel, rim),
        out_shape=[packed, packed],
        in_specs=[vmem],
        out_specs=[vmem] * 2,
        compiler_params=params,
        name="pack",
    )(wave)
    first = lax.ppermute(first, ("rcv", "freq"), around(n_rcv, n_freq, -1))
    second = lax.ppermute(second, ("rcv", "freq"), around(n_rcv, n_freq, 1))

    square = (2 * width, 2 * width)
    rcv_full, rcv_high, rcv_low, found = pl.pallas_call(
        functools.partial(rcv_operator_kernel, lateral),
        out_shape=[
            jax.ShapeDtypeStruct(square, F32),
            jax.ShapeDtypeStruct(square, BF16),
            jax.ShapeDtypeStruct(square, BF16),
            jax.ShapeDtypeStruct((2, (chunks + 1) * 2 * width // TILE, width), F32),
        ],
        in_specs=[vmem] * 2,
        out_specs=[vmem] * 4,
        scratch_shapes=[pltpu.VMEM((2, width, op_table.shape[1]), F32), pltpu.VMEM((2,) + square, F32)],
        compiler_params=params,
        cost_estimate=cost,
        name="rcv_operator",
    )(*tables)
    field, one, two, image = pl.pallas_call(
        functools.partial(receiver_kernel, rim),
        out_shape=[
            jax.ShapeDtypeStruct((2, rows, width), F32),
            jax.ShapeDtypeStruct((2, edge, width), F32),
            jax.ShapeDtypeStruct((2, edge, width), F32),
            jax.ShapeDtypeStruct((1, width), F32),
        ],
        in_specs=[vmem] * 6,
        out_specs=[vmem] * 4,
        compiler_params=params,
        name="receivers",
    )(wave, first, second, rcv_full, rcv_high, rcv_low)

    if n_freq == 2:
        other = lax.ppermute(one, "freq", [(0, 1), (1, 0)])
        image = image + jnp.where(lax.axis_index("src") % 2 == 0, other[0, :1], other[0, edge - 1 :])
    else:
        image = lax.psum(image, "freq")
    one = lax.ppermute(one, "src", [(i, i + 1 if i % 2 == 0 else i - 1) for i in range(n_src)])
    if n_src == 4:
        pairs = [(i * n_freq + f, (i ^ (2 + f % 2)) * n_freq + f) for i in range(n_src) for f in range(n_freq)]
        far = lax.ppermute(image, ("src", "freq"), pairs)
        if n_freq > 2:
            far = jnp.where(lax.axis_index("freq") < 2, far, 0.0)
    two = lax.ppermute(two, ("src", "freq"), between(n_src, n_freq))
    one, found = lax.optimization_barrier((one, found))
    src_high, src_low = pl.pallas_call(
        functools.partial(src_operator_kernel, lateral, op_table.shape[2]),
        out_shape=[jax.ShapeDtypeStruct((chunks,) + square, BF16)] * 2,
        in_specs=[vmem],
        out_specs=[vmem] * 2,
        scratch_shapes=[pltpu.VMEM((2,) + square, F32)],
        compiler_params=params,
        cost_estimate=pl.CostEstimate(flops=2**20, bytes_accessed=2**10, transcendentals=0),
        name="src_operator",
    )(found)
    if n_src == 4:
        up = lax.axis_index("src") % 2 == 0
        from_one = jnp.where(up, one[0, edge - 1 :], one[0, :1])
        near, src_high = lax.optimization_barrier((from_one + far, src_high))
        if n_freq == 2:
            images = [image, near, lax.ppermute(near, "freq", [(0, 1), (1, 0)])]
        else:
            images = [image, lax.psum(near, "freq")]
    else:
        images = [lax.psum(image, "src")]
    sunk, image = pl.pallas_call(
        source_kernel,
        out_shape=[jax.ShapeDtypeStruct((2, rows, width), F32), jax.ShapeDtypeStruct((1, width), F32)],
        in_specs=[vmem] * (5 + len(images)),
        out_specs=[vmem] * 2,
        compiler_params=params,
        name="sources",
    )(field, two, one, src_high, src_low, *images)
    return sunk.reshape(wavefield.shape), image.reshape(width)


def solution(mesh):
    in_specs = (P(None, "freq", "src", "rcv"), P(), P(), P(), P(), P("freq"))
    out_specs = (P(None, "freq", "src", "rcv"), P("rcv"))
    return jax.shard_map(body, mesh=mesh, in_specs=in_specs, out_specs=out_specs, check_vma=False)
```

```python
import functools

import jax
import jax.numpy as jnp
from jax import lax
from jax.experimental import pallas as pl
from jax.experimental.pallas import tpu as pltpu
from jax.sharding import PartitionSpec as P

SUBSTEPS = 4
TILE = 16
VMEM_LIMIT = 32 * 1024 * 1024
F32 = jnp.float32
BF16 = jnp.bfloat16


def halves(value):
    high = value.astype(BF16)
    low = (value - high.astype(F32)).astype(BF16)
    return high, low


def dot(left, right):
    return jnp.dot(left, right, preferred_element_type=F32)


def dot3(left, right):
    left_high, left_low = left
    right_high, right_low = right
    return dot(left_high, right_high) + (dot(left_high, right_low) + dot(left_low, right_high))


def complex_product(left, right):
    first = dot3(halves(left[0]), halves(right[0]))
    second = dot3(halves(left[1]), halves(right[1]))
    third = dot3(halves(left[0] + left[1]), halves(right[0] + right[1]))
    return first - second, third - first - second


def tile_taps(lateral_tiles, starts, window, small_ref, table_ref, table):
    count = window // TILE
    slots = (small_ref.shape[0] - 2) // 2
    tiles = velocities = small_ref.shape[1]
    entries, taps = table_ref.shape[2], table_ref.shape[0]
    place = lax.broadcasted_iota(jnp.int32, (count, tiles), 0)
    place = place - jnp.where(place >= count - count // 4, count, 0)
    tile = jnp.concatenate([start // TILE + place for start in starts], axis=0)
    lane = lax.broadcasted_iota(jnp.int32, tile.shape, 1)
    velocity = jnp.sum(jnp.where(lane == tile, small_ref[:1], 0.0), axis=1, keepdims=True)
    inside = jnp.logical_and(tile[:, :1] >= 0, tile[:, :1] < lateral_tiles).astype(F32)
    chosen = lax.broadcasted_iota(jnp.int32, (slots, velocities), 0).astype(F32) == small_ref[1:2, :1]
    index = jnp.sum(jnp.where(chosen, small_ref[2 : 2 + slots], 0.0), axis=0, keepdims=True)
    weight = jnp.sum(jnp.where(chosen, small_ref[2 + slots :], 0.0), axis=0, keepdims=True)
    rows = tile.shape[0]
    hit = lax.broadcasted_iota(jnp.int32, (rows, velocities), 1).astype(F32) == velocity
    index = jnp.sum(jnp.where(hit, index, 0.0), axis=1, keepdims=True)
    weight = jnp.sum(jnp.where(hit, weight, 0.0), axis=1, keepdims=True)
    entry = lax.broadcasted_iota(jnp.int32, (rows, entries), 1).astype(F32)
    mix = jnp.where(entry == index, 1.0 - weight, 0.0) + jnp.where(entry == index + 1.0, weight, 0.0)
    mix = mix * inside
    table[...] = jnp.zeros_like(table)
    found = []
    for part in range(2):
        table[part, :taps, :] = table_ref[:, part, :]
        found.append(
            lax.dot_general(
                mix, table[part], (((1,), (1,)), ((), ())), precision=lax.Precision.HIGHEST, preferred_element_type=F32
            )
        )
    return found


def fill_band(found, first, taps, band):
    window = band.shape[1]
    for position in range(window // TILE):
        shift = (position * TILE - taps // 2) % window
        for part in range(2):
            row = found[part][first + position : first + position + 1]
            spread = jnp.broadcast_to(row, (TILE, row.shape[1]))
            slanted = pltpu.roll(spread, 0, 1, stride=1, stride_axis=0)
            wide = jnp.concatenate([slanted, jnp.zeros((TILE, window - slanted.shape[1]), F32)], axis=1)
            band[part, pl.ds(position * TILE, TILE), :] = pltpu.roll(wide, shift, 1)


def four_substeps(start, lateral, once):
    window = once[0].shape[0]
    width = window // 2
    twice = complex_product(once, once)
    four = complex_product((twice[0][:width], twice[1][:width]), twice)
    place = lax.broadcasted_iota(jnp.int32, (width, window), 1)
    cell = start + jnp.where(place < window - width // 2, place, place - window)
    inside = jnp.logical_and(cell >= 0, cell < lateral)
    return jnp.where(inside, four[0], 0.0), jnp.where(inside, four[1], 0.0)


def groups_of(rows, width, rim):
    count = width // rim
    step = -(-rows // (8 * count)) * 8
    return width // count, [(low, min(low + step, rows)) for low in range(0, rows, step)]


def pack_kernel(rim, wave_ref, one_ref, two_ref):
    rows, width = wave_ref.shape
    span, groups = groups_of(rows, width, rim)
    odd = lax.axis_index("freq") % 2 == 1
    lane = lax.broadcasted_iota(jnp.int32, one_ref.shape, 1)
    packed = []
    for sign in (1, -1):
        message = wave_ref[: groups[0][1]]
        for index, (low, high) in enumerate(groups[1:], 1):
            count = high - low
            place = lane[:count] if sign == 1 else width - 1 - lane[:count]
            moved = pltpu.roll(wave_ref[low:high], sign * index * span % width, 1)
            top = jnp.where(place // span == index, moved, message[:count])
            message = top if count == message.shape[0] else jnp.concatenate([top, message[count:]], axis=0)
        packed.append(message)
    one_ref[...] = jnp.where(odd, packed[1], packed[0])
    two_ref[...] = jnp.where(odd, packed[0], packed[1])


def rcv_operator_kernel(
    lateral, small_ref, table_ref, full_ref, high_ref, low_ref, found_ref, table, band
):
    width = full_ref.shape[1] // 2
    taps, window = table_ref.shape[0], 2 * width
    chunks = found_ref.shape[1] * TILE // window - 1
    starts = [lax.axis_index("rcv") * width]
    starts += [(lax.axis_index("src") * chunks + chunk) * width for chunk in range(chunks)]
    found = tile_taps(lateral // TILE, starts, window, small_ref, table_ref, table)
    fill_band(found, 0, taps, band)
    for part in range(2):
        found_ref[part] = found[part]
    real, imag = four_substeps(starts[0], lateral, (band[0], band[1]))
    turned = jnp.concatenate([real.T, imag.T], axis=1)
    full_ref[...] = turned
    high_ref[...], low_ref[...] = halves(turned)


def src_operator_kernel(lateral, taps, found_ref, high_ref, low_ref, band):
    chunks, width = high_ref.shape[0], high_ref.shape[2] // 2
    found = (found_ref[0], found_ref[1])
    for chunk in range(chunks):
        start = (lax.axis_index("src") * chunks + chunk) * width
        fill_band(found, (chunk + 1) * 2 * width // TILE, taps, band)
        real, imag = four_substeps(start, lateral, (band[0], band[1]))
        high_ref[chunk], low_ref[chunk] = halves(jnp.concatenate([real, imag], axis=0))


def receiver_kernel(rim, wave_ref, first_ref, second_ref, full_ref, high_ref, low_ref, sunk_ref, one_ref, two_ref, image_ref):
    rows, width = sunk_ref.shape[1], sunk_ref.shape[2]
    half = width // 2
    span, groups = groups_of(2 * rows, width, rim)
    odd = lax.axis_index("freq") % 2 == 1
    before = jnp.where(odd, first_ref[...], second_ref[...])
    after = jnp.where(odd, second_ref[...], first_ref[...])
    halos = []
    for index, (low, high) in enumerate(groups):
        left, right = after[: high - low], before[: high - low]
        if index:
            left = pltpu.roll(left, -index * span % width, 1)
            right = pltpu.roll(right, index * span % width, 1)
        lane = lax.broadcasted_iota(jnp.int32, left.shape, 1)
        halos.append(jnp.where(lane < half, left, right))
    extended = jnp.concatenate([wave_ref[...], jnp.concatenate(halos, axis=0)], axis=1)
    full = dot3(halves(extended), (high_ref[...], low_ref[...]))
    real = full[:rows, :width] - full[rows:, width:]
    imag = full[:rows, width:] + full[rows:, :width]
    sunk_ref[0] = real
    sunk_ref[1] = imag
    chunks = rows // width
    ahead = lax.axis_index("src") * chunks - lax.axis_index("rcv")
    line = lax.broadcasted_iota(jnp.int32, (width, 2 * width), 0)
    image = jnp.zeros((1, width), F32)
    for chunk in range(chunks):
        away = ahead + chunk
        beside = jnp.logical_or(
            jnp.logical_and(away == 1, line < half), jnp.logical_and(away == -1, line >= half)
        )
        weights = jnp.where(away == 0, full_ref[:width], jnp.where(beside, full_ref[width:], 0.0))
        piece = slice(chunk * width, (chunk + 1) * width)
        terms = weights[:, :width] * real[piece] - weights[:, width:] * imag[piece]
        image = image + jnp.sum(terms, axis=0, keepdims=True)
    image_ref[...] = image
    edge = one_ref.shape[1]
    row = lax.broadcasted_iota(jnp.int32, (edge, width), 0)
    head = (jnp.where(row == edge - 1, image, real[:edge]), imag[:edge])
    tail = (jnp.where(row == 0, image, real[rows - edge :]), imag[rows - edge :])
    up = lax.axis_index("src") % 2 == 0
    for part in range(2):
        one_ref[part] = jnp.where(up, tail[part], head[part])
        two_ref[part] = jnp.where(up, head[part], tail[part])


def source_kernel(field_ref, two_ref, one_ref, high_ref, low_ref, out_ref):
    rows, width = field_ref.shape[1], field_ref.shape[2]
    half = width // 2
    chunks = rows // width
    edge = one_ref.shape[1]
    up = lax.axis_index("src") % 2 == 0
    gap = jnp.zeros((half - edge, width), F32)
    for chunk in range(chunks):
        low, high = chunk * width, (chunk + 1) * width
        extended = []
        for part in range(2):
            if chunk + 1 < chunks:
                after = field_ref[part, high : high + half]
            else:
                after = jnp.concatenate([jnp.where(up, one_ref[part], two_ref[part]), gap], axis=0)
            if chunk > 0:
                before = field_ref[part, low - half : low]
            else:
                before = jnp.concatenate([gap, jnp.where(up, two_ref[part], one_ref[part])], axis=0)
            extended.append(jnp.concatenate([field_ref[part, low:high], after, before], axis=0))
        full = dot3((high_ref[chunk], low_ref[chunk]), halves(jnp.concatenate(extended, axis=1)))
        out_ref[0, low:high] = full[:width, :width] - full[width:, width:]
        out_ref[1, low:high] = full[:width, width:] + full[width:, :width]


def store_kernel(sunk_ref, two_ref, *rest):
    *image_refs, sunk_hbm, image_hbm, image_ref, sems = rest
    sunk_copy = pltpu.make_async_copy(sunk_ref, sunk_hbm, sems.at[0])
    sunk_copy.start()
    image = functools.reduce(jnp.add, [ref[...] for ref in image_refs])
    if len(image_refs) > 1:
        at, edge = lax.axis_index("src"), two_ref.shape[1]
        from_two = jnp.where(at % 2 == 0, two_ref[0, :1], two_ref[0, edge - 1 :])
        image = image + jnp.where(jnp.logical_and(at > 0, at < lax.axis_size("src") - 1), from_two, 0.0)
    image_ref[...] = image
    image_copy = pltpu.make_async_copy(image_ref, image_hbm, sems.at[1])
    image_copy.start()
    sunk_copy.wait()
    image_copy.wait()


def around(rcv, freq, sign):
    pairs = []
    for at in range(rcv):
        for slot in range(freq):
            target = at + (sign if slot % 2 == 0 else -sign)
            to_slot = slot
            if not 0 <= target < rcv:
                target, to_slot = at, slot ^ 1
            pairs.append((at * freq + slot, target * freq + to_slot))
    return pairs


def between(src, freq):
    pairs = []
    for at in range(src):
        target = at - 1 if at % 2 == 0 else at + 1
        for slot in range(freq):
            ends = not 0 <= target < src
            pairs.append((at * freq + slot, at * freq + (slot ^ 1) if ends else target * freq + slot))
    return pairs


def far_pairs(freq):
    pairs = []
    for slot in range(0, freq, 2):
        moves = {
            (1, 0): (1, 1), (1, 1): (3, 0), (3, 0): (1, 0),
            (0, 0): (2, 1), (2, 1): (2, 0), (2, 0): (0, 0),
            (0, 1): (3, 1), (3, 1): (0, 1),
        }
        for (at, side), (to, to_side) in sorted(moves.items()):
            pairs.append((at * freq + slot + side, to * freq + slot + to_side))
    return pairs


def body(wavefield, op_table, vel_index, interp_index, interp_weight, freq_perm):
    rows, width = wavefield.shape[2], wavefield.shape[3]
    n_src, n_rcv, n_freq = (lax.axis_size(axis) for axis in ("src", "rcv", "freq"))
    lateral = width * n_rcv
    rim = SUBSTEPS * (op_table.shape[2] // 2)
    edge = -(-(rim + 1) // 8) * 8
    half = width // 2
    chunks = rows // width
    wave = wavefield.reshape(2 * rows, width)

    vmem = pl.BlockSpec(memory_space=pltpu.VMEM)
    anywhere = pl.BlockSpec(memory_space=pltpu.HBM)
    params = pltpu.CompilerParams(vmem_limit_bytes=VMEM_LIMIT)
    cost = pl.CostEstimate(flops=6 * 2**28, bytes_accessed=2**20, transcendentals=0)

    small = max(vel_index.shape[0], interp_index.shape[0], width)
    rows_of = lambda a: jnp.pad(a.astype(F32), ((0, 0), (0, small - a.shape[1])))
    tables = [
        jnp.concatenate(
            [rows_of(vel_index.reshape(1, -1)), jnp.pad(freq_perm, (0, small - 1)).astype(F32).reshape(1, -1), rows_of(interp_index.T), rows_of(interp_weight.T)]
        ),
        op_table.transpose(2, 0, 1),
    ]
    _, groups = groups_of(2 * rows, width, rim)
    packed = jax.ShapeDtypeStruct((groups[0][1], width), F32)
    first, second = pl.pallas_call(
        functools.partial(pack_kernel, rim),
        out_shape=[packed, packed],
        in_specs=[vmem],
        out_specs=[vmem] * 2,
        compiler_params=params,
        name="pack",
    )(wave)
    first = lax.ppermute(first, ("rcv", "freq"), around(n_rcv, n_freq, -1))
    second = lax.ppermute(second, ("rcv", "freq"), around(n_rcv, n_freq, 1))

    square = (2 * width, 2 * width)
    rcv_full, rcv_high, rcv_low, found = pl.pallas_call(
        functools.partial(rcv_operator_kernel, lateral),
        out_shape=[
            jax.ShapeDtypeStruct(square, F32),
            jax.ShapeDtypeStruct(square, BF16),
            jax.ShapeDtypeStruct(square, BF16),
            jax.ShapeDtypeStruct((2, (chunks + 1) * 2 * width // TILE, width), F32),
        ],
        in_specs=[vmem] * 2,
        out_specs=[vmem] * 4,
        scratch_shapes=[pltpu.VMEM((2, width, op_table.shape[1]), F32), pltpu.VMEM((2,) + square, F32)],
        compiler_params=params,
        cost_estimate=cost,
        name="rcv_operator",
    )(*tables)
    field, one, two, image = pl.pallas_call(
        functools.partial(receiver_kernel, rim),
        out_shape=[
            jax.ShapeDtypeStruct((2, rows, width), F32),
            jax.ShapeDtypeStruct((2, edge, width), F32),
            jax.ShapeDtypeStruct((2, edge, width), F32),
            jax.ShapeDtypeStruct((1, width), F32),
        ],
        in_specs=[vmem] * 6,
        out_specs=[vmem] * 4,
        compiler_params=params,
        name="receivers",
    )(wave, first, second, rcv_full, rcv_high, rcv_low)

    if n_freq == 2:
        other = lax.ppermute(one, "freq", [(0, 1), (1, 0)])
        image = image + jnp.where(lax.axis_index("src") % 2 == 0, other[0, :1], other[0, edge - 1 :])
    else:
        image = lax.psum(image, "freq")
    one = lax.ppermute(one, "src", [(i, i + 1 if i % 2 == 0 else i - 1) for i in range(n_src)])
    up = lax.axis_index("src") % 2 == 0
    if n_src == 4:
        far = lax.ppermute(image, ("src", "freq"), far_pairs(n_freq))
        two = lax.dynamic_update_slice(two, image[None], (0, jnp.where(up, edge - 1, 0), 0))
    two = lax.ppermute(two, ("src", "freq"), between(n_src, n_freq))
    one, found = lax.optimization_barrier((one, found))
    src_high, src_low = pl.pallas_call(
        functools.partial(src_operator_kernel, lateral, op_table.shape[2]),
        out_shape=[jax.ShapeDtypeStruct((chunks,) + square, BF16)] * 2,
        in_specs=[vmem],
        out_specs=[vmem] * 2,
        scratch_shapes=[pltpu.VMEM((2,) + square, F32)],
        compiler_params=params,
        cost_estimate=pl.CostEstimate(flops=2**20, bytes_accessed=2**10, transcendentals=0),
        name="src_operator",
    )(found)
    if n_src == 4:
        at, slot = lax.axis_index("src"), lax.axis_index("freq")
        from_one = jnp.where(up, one[0, edge - 1 :], one[0, :1])
        other = jnp.logical_or(jnp.logical_and(at == 1, slot == 1), jnp.logical_and(at == 2, slot == 0))
        from_far = jnp.where(jnp.logical_or(other, slot > 1), 0.0, far)
        near, src_high = lax.optimization_barrier((from_one + from_far, src_high))
        if n_freq == 2:
            images = [image, near, lax.ppermute(near, "freq", [(0, 1), (1, 0)])]
        else:
            images = [image, lax.psum(near, "freq")]
    else:
        images = [lax.psum(image, "src")]
    sunk = pl.pallas_call(
        source_kernel,
        out_shape=jax.ShapeDtypeStruct((2, rows, width), F32),
        in_specs=[vmem] * 5,
        out_specs=vmem,
        compiler_params=params,
        cost_estimate=cost,
        name="sources",
    )(field, two, one, src_high, src_low)
    sunk, image = pl.pallas_call(
        store_kernel,
        out_shape=[jax.ShapeDtypeStruct((2, rows, width), F32), jax.ShapeDtypeStruct((1, width), F32)],
        in_specs=[vmem] * (2 + len(images)),
        out_specs=[pl.BlockSpec(memory_space=pl.ANY)] * 2,
        scratch_shapes=[pltpu.VMEM((1, width), F32), pltpu.SemaphoreType.DMA((2,))],
        compiler_params=params,
        name="store",
    )(sunk, two, *images)
    return sunk.reshape(wavefield.shape), image.reshape(width)


def solution(mesh):
    in_specs = (P(None, "freq", "src", "rcv"), P(), P(), P(), P(), P("freq"))
    out_specs = (P(None, "freq", "src", "rcv"), P("rcv"))
    return jax.shard_map(body, mesh=mesh, in_specs=in_specs, out_specs=out_specs, check_vma=False)
```

```python
import functools

import jax
import jax.numpy as jnp
from jax import lax
from jax.experimental import pallas as pl
from jax.experimental.pallas import tpu as pltpu
from jax.sharding import PartitionSpec as P

SUBSTEPS = 4
TILE = 16
VMEM_LIMIT = 32 * 1024 * 1024
F32 = jnp.float32
BF16 = jnp.bfloat16


def halves(value):
    high = value.astype(BF16)
    low = (value - high.astype(F32)).astype(BF16)
    return high, low


def dot(left, right):
    return jnp.dot(left, right, preferred_element_type=F32)


def dot3(left, right):
    left_high, left_low = left
    right_high, right_low = right
    return dot(left_high, right_high) + (dot(left_high, right_low) + dot(left_low, right_high))


def complex_product(left, right):
    first = dot3(halves(left[0]), halves(right[0]))
    second = dot3(halves(left[1]), halves(right[1]))
    third = dot3(halves(left[0] + left[1]), halves(right[0] + right[1]))
    return first - second, third - first - second


def tile_taps(lateral_tiles, starts, window, small_ref, table_ref, table):
    count = window // TILE
    slots = (small_ref.shape[0] - 2) // 2
    tiles = velocities = small_ref.shape[1]
    entries, taps = table_ref.shape[2], table_ref.shape[0]
    place = lax.broadcasted_iota(jnp.int32, (count, tiles), 0)
    place = place - jnp.where(place >= count - count // 4, count, 0)
    tile = jnp.concatenate([start // TILE + place for start in starts], axis=0)
    lane = lax.broadcasted_iota(jnp.int32, tile.shape, 1)
    velocity = jnp.sum(jnp.where(lane == tile, small_ref[:1], 0.0), axis=1, keepdims=True)
    inside = jnp.logical_and(tile[:, :1] >= 0, tile[:, :1] < lateral_tiles).astype(F32)
    chosen = lax.broadcasted_iota(jnp.int32, (slots, velocities), 0).astype(F32) == small_ref[1:2, :1]
    index = jnp.sum(jnp.where(chosen, small_ref[2 : 2 + slots], 0.0), axis=0, keepdims=True)
    weight = jnp.sum(jnp.where(chosen, small_ref[2 + slots :], 0.0), axis=0, keepdims=True)
    rows = tile.shape[0]
    hit = lax.broadcasted_iota(jnp.int32, (rows, velocities), 1).astype(F32) == velocity
    index = jnp.sum(jnp.where(hit, index, 0.0), axis=1, keepdims=True)
    weight = jnp.sum(jnp.where(hit, weight, 0.0), axis=1, keepdims=True)
    entry = lax.broadcasted_iota(jnp.int32, (rows, entries), 1).astype(F32)
    mix = jnp.where(entry == index, 1.0 - weight, 0.0) + jnp.where(entry == index + 1.0, weight, 0.0)
    mix = mix * inside
    table[...] = jnp.zeros_like(table)
    found = []
    for part in range(2):
        table[part, :taps, :] = table_ref[:, part, :]
        found.append(
            lax.dot_general(
                mix, table[part], (((1,), (1,)), ((), ())), precision=lax.Precision.HIGHEST, preferred_element_type=F32
            )
        )
    return found


def fill_band(found, first, taps, band):
    window = band.shape[1]
    for position in range(window // TILE):
        shift = (position * TILE - taps // 2) % window
        for part in range(2):
            row = found[part][first + position : first + position + 1]
            spread = jnp.broadcast_to(row, (TILE, row.shape[1]))
            slanted = pltpu.roll(spread, 0, 1, stride=1, stride_axis=0)
            wide = jnp.concatenate([slanted, jnp.zeros((TILE, window - slanted.shape[1]), F32)], axis=1)
            band[part, pl.ds(position * TILE, TILE), :] = pltpu.roll(wide, shift, 1)


def four_substeps(start, lateral, once):
    window = once[0].shape[0]
    width = window // 2
    twice = complex_product(once, once)
    four = complex_product((twice[0][:width], twice[1][:width]), twice)
    place = lax.broadcasted_iota(jnp.int32, (width, window), 1)
    cell = start + jnp.where(place < window - width // 2, place, place - window)
    inside = jnp.logical_and(cell >= 0, cell < lateral)
    return jnp.where(inside, four[0], 0.0), jnp.where(inside, four[1], 0.0)


def groups_of(rows, width, rim):
    count = width // rim
    step = -(-rows // (8 * count)) * 8
    return width // count, [(low, min(low + step, rows)) for low in range(0, rows, step)]


def pack_kernel(rim, wave_ref, one_ref, two_ref):
    rows, width = wave_ref.shape
    span, groups = groups_of(rows, width, rim)
    odd = lax.axis_index("freq") % 2 == 1
    lane = lax.broadcasted_iota(jnp.int32, one_ref.shape, 1)
    packed = []
    for sign in (1, -1):
        message = wave_ref[: groups[0][1]]
        for index, (low, high) in enumerate(groups[1:], 1):
            count = high - low
            place = lane[:count] if sign == 1 else width - 1 - lane[:count]
            moved = pltpu.roll(wave_ref[low:high], sign * index * span % width, 1)
            top = jnp.where(place // span == index, moved, message[:count])
            message = top if count == message.shape[0] else jnp.concatenate([top, message[count:]], axis=0)
        packed.append(message)
    one_ref[...] = jnp.where(odd, packed[1], packed[0])
    two_ref[...] = jnp.where(odd, packed[0], packed[1])


def rcv_operator_kernel(
    lateral, small_ref, table_ref, full_ref, high_ref, low_ref, found_ref, table, band
):
    width = full_ref.shape[1] // 2
    taps, window = table_ref.shape[0], 2 * width
    chunks = found_ref.shape[1] * TILE // window - 1
    starts = [lax.axis_index("rcv") * width]
    starts += [(lax.axis_index("src") * chunks + chunk) * width for chunk in range(chunks)]
    found = tile_taps(lateral // TILE, starts, window, small_ref, table_ref, table)
    fill_band(found, 0, taps, band)
    for part in range(2):
        found_ref[part] = found[part]
    real, imag = four_substeps(starts[0], lateral, (band[0], band[1]))
    turned = jnp.concatenate([real.T, imag.T], axis=1)
    full_ref[...] = turned
    high_ref[...], low_ref[...] = halves(turned)


def src_operator_kernel(lateral, taps, found_ref, high_ref, low_ref, band):
    chunks, width = high_ref.shape[0], high_ref.shape[2] // 2
    found = (found_ref[0], found_ref[1])
    for chunk in range(chunks):
        start = (lax.axis_index("src") * chunks + chunk) * width
        fill_band(found, (chunk + 1) * 2 * width // TILE, taps, band)
        real, imag = four_substeps(start, lateral, (band[0], band[1]))
        high_ref[chunk], low_ref[chunk] = halves(jnp.concatenate([real, imag], axis=0))


def receiver_kernel(rim, wave_ref, first_ref, second_ref, full_ref, high_ref, low_ref, sunk_ref, one_ref, two_ref, image_ref):
    rows, width = sunk_ref.shape[1], sunk_ref.shape[2]
    half = width // 2
    span, groups = groups_of(2 * rows, width, rim)
    odd = lax.axis_index("freq") % 2 == 1
    before = jnp.where(odd, first_ref[...], second_ref[...])
    after = jnp.where(odd, second_ref[...], first_ref[...])
    halos = []
    for index, (low, high) in enumerate(groups):
        left, right = after[: high - low], before[: high - low]
        if index:
            left = pltpu.roll(left, -index * span % width, 1)
            right = pltpu.roll(right, index * span % width, 1)
        lane = lax.broadcasted_iota(jnp.int32, left.shape, 1)
        halos.append(jnp.where(lane < half, left, right))
    extended = jnp.concatenate([wave_ref[...], jnp.concatenate(halos, axis=0)], axis=1)
    full = dot3(halves(extended), (high_ref[...], low_ref[...]))
    real = full[:rows, :width] - full[rows:, width:]
    imag = full[:rows, width:] + full[rows:, :width]
    sunk_ref[0] = real
    sunk_ref[1] = imag
    chunks = rows // width
    ahead = lax.axis_index("src") * chunks - lax.axis_index("rcv")
    line = lax.broadcasted_iota(jnp.int32, (width, 2 * width), 0)
    image = jnp.zeros((1, width), F32)
    for chunk in range(chunks):
        away = ahead + chunk
        beside = jnp.logical_or(
            jnp.logical_and(away == 1, line < half), jnp.logical_and(away == -1, line >= half)
        )
        weights = jnp.where(away == 0, full_ref[:width], jnp.where(beside, full_ref[width:], 0.0))
        piece = slice(chunk * width, (chunk + 1) * width)
        terms = weights[:, :width] * real[piece] - weights[:, width:] * imag[piece]
        image = image + jnp.sum(terms, axis=0, keepdims=True)
    image_ref[...] = image
    edge = one_ref.shape[1]
    row = lax.broadcasted_iota(jnp.int32, (edge, width), 0)
    head = (jnp.where(row == edge - 1, image, real[:edge]), imag[:edge])
    tail = (jnp.where(row == 0, image, real[rows - edge :]), imag[rows - edge :])
    up = lax.axis_index("src") % 2 == 0
    for part in range(2):
        one_ref[part] = jnp.where(up, tail[part], head[part])
        two_ref[part] = jnp.where(up, head[part], tail[part])


def source_kernel(field_ref, two_ref, one_ref, high_ref, low_ref, out_ref):
    rows, width = field_ref.shape[1], field_ref.shape[2]
    half = width // 2
    chunks = rows // width
    edge = one_ref.shape[1]
    up = lax.axis_index("src") % 2 == 0
    gap = jnp.zeros((half - edge, width), F32)
    for chunk in range(chunks):
        low, high = chunk * width, (chunk + 1) * width
        extended = []
        for part in range(2):
            if chunk + 1 < chunks:
                after = field_ref[part, high : high + half]
            else:
                after = jnp.concatenate([jnp.where(up, one_ref[part], two_ref[part]), gap], axis=0)
            if chunk > 0:
                before = field_ref[part, low - half : low]
            else:
                before = jnp.concatenate([gap, jnp.where(up, two_ref[part], one_ref[part])], axis=0)
            extended.append(jnp.concatenate([field_ref[part, low:high], after, before], axis=0))
        full = dot3((high_ref[chunk], low_ref[chunk]), halves(jnp.concatenate(extended, axis=1)))
        out_ref[0, low:high] = full[:width, :width] - full[width:, width:]
        out_ref[1, low:high] = full[:width, width:] + full[width:, :width]


def store_kernel(sunk_ref, two_ref, *rest):
    *image_refs, sunk_hbm, image_hbm, image_ref, sems = rest
    sunk_copy = pltpu.make_async_copy(sunk_ref, sunk_hbm, sems.at[0])
    sunk_copy.start()
    image = functools.reduce(jnp.add, [ref[...] for ref in image_refs])
    if len(image_refs) > 1:
        at, edge = lax.axis_index("src"), two_ref.shape[1]
        from_two = jnp.where(at % 2 == 0, two_ref[0, :1], two_ref[0, edge - 1 :])
        image = image + jnp.where(jnp.logical_and(at > 0, at < lax.axis_size("src") - 1), from_two, 0.0)
    image_ref[...] = image
    image_copy = pltpu.make_async_copy(image_ref, image_hbm, sems.at[1])
    image_copy.start()
    sunk_copy.wait()
    image_copy.wait()


def around(rcv, freq, sign):
    pairs = []
    for at in range(rcv):
        for slot in range(freq):
            target = at + (sign if slot % 2 == 0 else -sign)
            to_slot = slot
            if not 0 <= target < rcv:
                target, to_slot = at, slot ^ 1
            pairs.append((at * freq + slot, target * freq + to_slot))
    return pairs


def between(src, freq):
    pairs = []
    for at in range(src):
        target = at - 1 if at % 2 == 0 else at + 1
        for slot in range(freq):
            ends = not 0 <= target < src
            pairs.append((at * freq + slot, at * freq + (slot ^ 1) if ends else target * freq + slot))
    return pairs


def far_pairs(freq):
    pairs = []
    for slot in range(0, freq, 2):
        moves = {
            (1, 0): (1, 1), (1, 1): (3, 0), (3, 0): (1, 0),
            (0, 0): (2, 0), (2, 0): (2, 1), (2, 1): (0, 0),
            (0, 1): (3, 1), (3, 1): (0, 1),
        }
        for (at, side), (to, to_side) in sorted(moves.items()):
            pairs.append((at * freq + slot + side, to * freq + slot + to_side))
    return pairs


def body(wavefield, op_table, vel_index, interp_index, interp_weight, freq_perm):
    rows, width = wavefield.shape[2], wavefield.shape[3]
    n_src, n_rcv, n_freq = (lax.axis_size(axis) for axis in ("src", "rcv", "freq"))
    lateral = width * n_rcv
    rim = SUBSTEPS * (op_table.shape[2] // 2)
    edge = -(-(rim + 1) // 8) * 8
    half = width // 2
    chunks = rows // width
    wave = wavefield.reshape(2 * rows, width)

    vmem = pl.BlockSpec(memory_space=pltpu.VMEM)
    anywhere = pl.BlockSpec(memory_space=pltpu.HBM)
    params = pltpu.CompilerParams(vmem_limit_bytes=VMEM_LIMIT)
    cost = pl.CostEstimate(flops=6 * 2**28, bytes_accessed=2**20, transcendentals=0)

    small = max(vel_index.shape[0], interp_index.shape[0], width)
    rows_of = lambda a: jnp.pad(a.astype(F32), ((0, 0), (0, small - a.shape[1])))
    tables = [
        jnp.concatenate(
            [rows_of(vel_index.reshape(1, -1)), jnp.pad(freq_perm, (0, small - 1)).astype(F32).reshape(1, -1), rows_of(interp_index.T), rows_of(interp_weight.T)]
        ),
        op_table.transpose(2, 0, 1),
    ]
    _, groups = groups_of(2 * rows, width, rim)
    packed = jax.ShapeDtypeStruct((groups[0][1], width), F32)
    first, second = pl.pallas_call(
        functools.partial(pack_kernel, rim),
        out_shape=[packed, packed],
        in_specs=[vmem],
        out_specs=[vmem] * 2,
        compiler_params=params,
        name="pack",
    )(wave)
    first = lax.ppermute(first, ("rcv", "freq"), around(n_rcv, n_freq, -1))
    second = lax.ppermute(second, ("rcv", "freq"), around(n_rcv, n_freq, 1))

    square = (2 * width, 2 * width)
    rcv_full, rcv_high, rcv_low, found = pl.pallas_call(
        functools.partial(rcv_operator_kernel, lateral),
        out_shape=[
            jax.ShapeDtypeStruct(square, F32),
            jax.ShapeDtypeStruct(square, BF16),
            jax.ShapeDtypeStruct(square, BF16),
            jax.ShapeDtypeStruct((2, (chunks + 1) * 2 * width // TILE, width), F32),
        ],
        in_specs=[vmem] * 2,
        out_specs=[vmem] * 4,
        scratch_shapes=[pltpu.VMEM((2, width, op_table.shape[1]), F32), pltpu.VMEM((2,) + square, F32)],
        compiler_params=params,
        cost_estimate=cost,
        name="rcv_operator",
    )(*tables)
    field, one, two, image = pl.pallas_call(
        functools.partial(receiver_kernel, rim),
        out_shape=[
            jax.ShapeDtypeStruct((2, rows, width), F32),
            jax.ShapeDtypeStruct((2, edge, width), F32),
            jax.ShapeDtypeStruct((2, edge, width), F32),
            jax.ShapeDtypeStruct((1, width), F32),
        ],
        in_specs=[vmem] * 6,
        out_specs=[vmem] * 4,
        compiler_params=params,
        name="receivers",
    )(wave, first, second, rcv_full, rcv_high, rcv_low)

    if n_freq == 2:
        other = lax.ppermute(one, "freq", [(0, 1), (1, 0)])
        image = image + jnp.where(lax.axis_index("src") % 2 == 0, other[0, :1], other[0, edge - 1 :])
    else:
        image = lax.psum(image, "freq")
    one = lax.ppermute(one, "src", [(i, i + 1 if i % 2 == 0 else i - 1) for i in range(n_src)])
    up = lax.axis_index("src") % 2 == 0
    if n_src == 4:
        far = lax.ppermute(image, ("src", "freq"), far_pairs(n_freq))
        two = lax.dynamic_update_slice(two, image[None], (0, jnp.where(up, edge - 1, 0), 0))
    two = lax.ppermute(two, ("src", "freq"), between(n_src, n_freq))
    one, found = lax.optimization_barrier((one, found))
    src_high, src_low = pl.pallas_call(
        functools.partial(src_operator_kernel, lateral, op_table.shape[2]),
        out_shape=[jax.ShapeDtypeStruct((chunks,) + square, BF16)] * 2,
        in_specs=[vmem],
        out_specs=[vmem] * 2,
        scratch_shapes=[pltpu.VMEM((2,) + square, F32)],
        compiler_params=params,
        cost_estimate=pl.CostEstimate(flops=2**20, bytes_accessed=2**10, transcendentals=0),
        name="src_operator",
    )(found)
    if n_src == 4:
        at, slot = lax.axis_index("src"), lax.axis_index("freq")
        from_one = jnp.where(up, one[0, edge - 1 :], one[0, :1])
        other = jnp.logical_or(jnp.logical_and(at == 1, slot == 1), jnp.logical_and(at == 2, slot == 1))
        from_far = jnp.where(jnp.logical_or(other, slot > 1), 0.0, far)
        near, src_high = lax.optimization_barrier((from_one + from_far, src_high))
        if n_freq == 2:
            images = [image, near, lax.ppermute(near, "freq", [(0, 1), (1, 0)])]
        else:
            images = [image, lax.psum(near, "freq")]
    else:
        images = [lax.psum(image, "src")]
    sunk = pl.pallas_call(
        source_kernel,
        out_shape=jax.ShapeDtypeStruct((2, rows, width), F32),
        in_specs=[vmem] * 5,
        out_specs=vmem,
        compiler_params=params,
        cost_estimate=cost,
        name="sources",
    )(field, two, one, src_high, src_low)
    sunk, image = pl.pallas_call(
        store_kernel,
        out_shape=[jax.ShapeDtypeStruct((2, rows, width), F32), jax.ShapeDtypeStruct((1, width), F32)],
        in_specs=[vmem] * (2 + len(images)),
        out_specs=[pl.BlockSpec(memory_space=pl.ANY)] * 2,
        scratch_shapes=[pltpu.VMEM((1, width), F32), pltpu.SemaphoreType.DMA((2,))],
        compiler_params=params,
        name="store",
    )(sunk, two, *images)
    return sunk.reshape(wavefield.shape), image.reshape(width)


def solution(mesh):
    in_specs = (P(None, "freq", "src", "rcv"), P(), P(), P(), P(), P("freq"))
    out_specs = (P(None, "freq", "src", "rcv"), P("rcv"))
    return jax.shard_map(body, mesh=mesh, in_specs=in_specs, out_specs=out_specs, check_vma=False)
```

```python
import functools

import jax
import jax.numpy as jnp
from jax import lax
from jax.experimental import pallas as pl
from jax.experimental.pallas import tpu as pltpu
from jax.sharding import PartitionSpec as P

SUBSTEPS = 4
TILE = 16
VMEM_LIMIT = 32 * 1024 * 1024
F32 = jnp.float32
BF16 = jnp.bfloat16


def halves(value):
    high = value.astype(BF16)
    low = (value - high.astype(F32)).astype(BF16)
    return high, low


def dot(left, right):
    return jnp.dot(left, right, preferred_element_type=F32)


def dot3(left, right):
    left_high, left_low = left
    right_high, right_low = right
    return dot(left_high, right_high) + (dot(left_high, right_low) + dot(left_low, right_high))


def complex_product(left, right):
    first = dot3(halves(left[0]), halves(right[0]))
    second = dot3(halves(left[1]), halves(right[1]))
    third = dot3(halves(left[0] + left[1]), halves(right[0] + right[1]))
    return first - second, third - first - second


def tile_taps(lateral_tiles, starts, window, small_ref, table_ref, table):
    count = window // TILE
    slots = (small_ref.shape[0] - 2) // 2
    tiles = velocities = small_ref.shape[1]
    entries, taps = table_ref.shape[2], table_ref.shape[0]
    place = lax.broadcasted_iota(jnp.int32, (count, tiles), 0)
    place = place - jnp.where(place >= count - count // 4, count, 0)
    tile = jnp.concatenate([start // TILE + place for start in starts], axis=0)
    lane = lax.broadcasted_iota(jnp.int32, tile.shape, 1)
    velocity = jnp.sum(jnp.where(lane == tile, small_ref[:1], 0.0), axis=1, keepdims=True)
    inside = jnp.logical_and(tile[:, :1] >= 0, tile[:, :1] < lateral_tiles).astype(F32)
    chosen = lax.broadcasted_iota(jnp.int32, (slots, velocities), 0).astype(F32) == small_ref[1:2, :1]
    index = jnp.sum(jnp.where(chosen, small_ref[2 : 2 + slots], 0.0), axis=0, keepdims=True)
    weight = jnp.sum(jnp.where(chosen, small_ref[2 + slots :], 0.0), axis=0, keepdims=True)
    rows = tile.shape[0]
    hit = lax.broadcasted_iota(jnp.int32, (rows, velocities), 1).astype(F32) == velocity
    index = jnp.sum(jnp.where(hit, index, 0.0), axis=1, keepdims=True)
    weight = jnp.sum(jnp.where(hit, weight, 0.0), axis=1, keepdims=True)
    entry = lax.broadcasted_iota(jnp.int32, (rows, entries), 1).astype(F32)
    mix = jnp.where(entry == index, 1.0 - weight, 0.0) + jnp.where(entry == index + 1.0, weight, 0.0)
    mix = mix * inside
    table[...] = jnp.zeros_like(table)
    found = []
    for part in range(2):
        table[part, :taps, :] = table_ref[:, part, :]
        found.append(
            lax.dot_general(
                mix, table[part], (((1,), (1,)), ((), ())), precision=lax.Precision.HIGHEST, preferred_element_type=F32
            )
        )
    return found


def fill_band(found, first, taps, band):
    window = band.shape[1]
    for position in range(window // TILE):
        shift = (position * TILE - taps // 2) % window
        for part in range(2):
            row = found[part][first + position : first + position + 1]
            spread = jnp.broadcast_to(row, (TILE, row.shape[1]))
            slanted = pltpu.roll(spread, 0, 1, stride=1, stride_axis=0)
            wide = jnp.concatenate([slanted, jnp.zeros((TILE, window - slanted.shape[1]), F32)], axis=1)
            band[part, pl.ds(position * TILE, TILE), :] = pltpu.roll(wide, shift, 1)


def four_substeps(start, lateral, once):
    window = once[0].shape[0]
    width = window // 2
    twice = complex_product(once, once)
    four = complex_product((twice[0][:width], twice[1][:width]), twice)
    place = lax.broadcasted_iota(jnp.int32, (width, window), 1)
    cell = start + jnp.where(place < window - width // 2, place, place - window)
    inside = jnp.logical_and(cell >= 0, cell < lateral)
    return jnp.where(inside, four[0], 0.0), jnp.where(inside, four[1], 0.0)


def groups_of(rows, width, rim):
    count = width // rim
    step = -(-rows // (8 * count)) * 8
    return width // count, [(low, min(low + step, rows)) for low in range(0, rows, step)]


def pack_kernel(rim, wave_ref, one_ref, two_ref):
    rows, width = wave_ref.shape
    span, groups = groups_of(rows, width, rim)
    odd = lax.axis_index("freq") % 2 == 1
    lane = lax.broadcasted_iota(jnp.int32, one_ref.shape, 1)
    packed = []
    for sign in (1, -1):
        message = wave_ref[: groups[0][1]]
        for index, (low, high) in enumerate(groups[1:], 1):
            count = high - low
            place = lane[:count] if sign == 1 else width - 1 - lane[:count]
            moved = pltpu.roll(wave_ref[low:high], sign * index * span % width, 1)
            top = jnp.where(place // span == index, moved, message[:count])
            message = top if count == message.shape[0] else jnp.concatenate([top, message[count:]], axis=0)
        packed.append(message)
    one_ref[...] = jnp.where(odd, packed[1], packed[0])
    two_ref[...] = jnp.where(odd, packed[0], packed[1])


def rcv_operator_kernel(
    lateral, small_ref, table_ref, full_ref, high_ref, low_ref, found_ref, table, band
):
    width = full_ref.shape[1] // 2
    taps, window = table_ref.shape[0], 2 * width
    chunks = found_ref.shape[1] * TILE // window - 1
    starts = [lax.axis_index("rcv") * width]
    starts += [(lax.axis_index("src") * chunks + chunk) * width for chunk in range(chunks)]
    found = tile_taps(lateral // TILE, starts, window, small_ref, table_ref, table)
    fill_band(found, 0, taps, band)
    for part in range(2):
        found_ref[part] = found[part]
    real, imag = four_substeps(starts[0], lateral, (band[0], band[1]))
    turned = jnp.concatenate([real.T, imag.T], axis=1)
    full_ref[...] = turned
    high_ref[...], low_ref[...] = halves(turned)


def src_operator_kernel(lateral, taps, found_ref, high_ref, low_ref, band):
    chunks, width = high_ref.shape[0], high_ref.shape[2] // 2
    found = (found_ref[0], found_ref[1])
    for chunk in range(chunks):
        start = (lax.axis_index("src") * chunks + chunk) * width
        fill_band(found, (chunk + 1) * 2 * width // TILE, taps, band)
        real, imag = four_substeps(start, lateral, (band[0], band[1]))
        high_ref[chunk], low_ref[chunk] = halves(jnp.concatenate([real, imag], axis=0))


def receiver_kernel(rim, wave_ref, first_ref, second_ref, full_ref, high_ref, low_ref, sunk_ref, one_ref, two_ref, image_ref):
    rows, width = sunk_ref.shape[1], sunk_ref.shape[2]
    half = width // 2
    span, groups = groups_of(2 * rows, width, rim)
    odd = lax.axis_index("freq") % 2 == 1
    before = jnp.where(odd, first_ref[...], second_ref[...])
    after = jnp.where(odd, second_ref[...], first_ref[...])
    halos = []
    for index, (low, high) in enumerate(groups):
        left, right = after[: high - low], before[: high - low]
        if index:
            left = pltpu.roll(left, -index * span % width, 1)
            right = pltpu.roll(right, index * span % width, 1)
        lane = lax.broadcasted_iota(jnp.int32, left.shape, 1)
        halos.append(jnp.where(lane < half, left, right))
    extended = jnp.concatenate([wave_ref[...], jnp.concatenate(halos, axis=0)], axis=1)
    full = dot3(halves(extended), (high_ref[...], low_ref[...]))
    real = full[:rows, :width] - full[rows:, width:]
    imag = full[:rows, width:] + full[rows:, :width]
    sunk_ref[0] = real
    sunk_ref[1] = imag
    chunks = rows // width
    ahead = lax.axis_index("src") * chunks - lax.axis_index("rcv")
    line = lax.broadcasted_iota(jnp.int32, (width, 2 * width), 0)
    image = jnp.zeros((1, width), F32)
    for chunk in range(chunks):
        away = ahead + chunk
        beside = jnp.logical_or(
            jnp.logical_and(away == 1, line < half), jnp.logical_and(away == -1, line >= half)
        )
        weights = jnp.where(away == 0, full_ref[:width], jnp.where(beside, full_ref[width:], 0.0))
        piece = slice(chunk * width, (chunk + 1) * width)
        terms = weights[:, :width] * real[piece] - weights[:, width:] * imag[piece]
        image = image + jnp.sum(terms, axis=0, keepdims=True)
    image_ref[...] = image
    edge = one_ref.shape[1]
    row = lax.broadcasted_iota(jnp.int32, (edge, width), 0)
    head = (jnp.where(row == edge - 1, image, real[:edge]), imag[:edge])
    tail = (jnp.where(row == 0, image, real[rows - edge :]), imag[rows - edge :])
    up = lax.axis_index("src") % 2 == 0
    for part in range(2):
        one_ref[part] = jnp.where(up, tail[part], head[part])
        two_ref[part] = jnp.where(up, head[part], tail[part])


def inner_kernel(field_ref, one_ref, high_ref, low_ref, out_ref, part_ref):
    rows, width = field_ref.shape[1], field_ref.shape[2]
    half = width // 2
    chunks = rows // width
    up = lax.axis_index("src") % 2 == 0
    gap = jnp.zeros((half - one_ref.shape[1], width), F32)
    for chunk in range(chunks):
        low, high = chunk * width, (chunk + 1) * width
        extended = []
        for part in range(2):
            if chunk + 1 < chunks:
                after = field_ref[part, high : high + half]
            else:
                after = jnp.concatenate([jnp.where(up, one_ref[part], 0.0), gap], axis=0)
            if chunk > 0:
                before = field_ref[part, low - half : low]
            else:
                before = jnp.concatenate([gap, jnp.where(up, 0.0, one_ref[part])], axis=0)
            extended.append(jnp.concatenate([field_ref[part, low:high], after, before], axis=0))
        full = dot3((high_ref[chunk], low_ref[chunk]), halves(jnp.concatenate(extended, axis=1)))
        part_ref[chunk] = full
        out_ref[0, low:high] = full[:width, :width] - full[width:, width:]
        out_ref[1, low:high] = full[:width, width:] + full[width:, :width]


def source_kernel(sunk_hbm, part_ref, two_ref, high_ref, low_ref, *rest):
    *image_refs, out_hbm, image_hbm, edge_ref, image_ref, sems = rest
    del sunk_hbm
    chunks, width = part_ref.shape[0], two_ref.shape[2]
    half, edge, span = width // 2, two_ref.shape[1], edge_ref.shape[1]
    at = lax.axis_index("src")
    up = at % 2 == 0
    inner = jnp.logical_and(at > 0, at < lax.axis_size("src") - 1)
    image = functools.reduce(jnp.add, [ref[...] for ref in image_refs])
    if len(image_refs) > 1:
        from_two = jnp.where(up, two_ref[0, :1], two_ref[0, edge - 1 :])
        image = image + jnp.where(inner, from_two, 0.0)
    image_ref[...] = image
    image_copy = pltpu.make_async_copy(image_ref, image_hbm, sems.at[0])
    image_copy.start()

    @pl.when(inner)
    def _():
        none = jnp.zeros((half, width), F32)
        gap = none[: half - edge]
        first, last = slice(0, span), slice(width - span, width)

        def pick(ref, columns):
            chosen = [
                jnp.concatenate([ref[chunk, :width, columns][rows], ref[chunk, width:, columns][rows]], axis=0)
                for chunk, rows in ((0, first), (chunks - 1, last))
            ]
            return jnp.where(up, *chosen)

        halo = []
        for part in range(2):
            before = jnp.concatenate([none, gap, two_ref[part]], axis=0)
            after = jnp.concatenate([two_ref[part], gap, none], axis=0)
            halo.append(jnp.where(up, before, after))
        beside = slice(width, 2 * width)
        operator = (pick(high_ref, beside), pick(low_ref, beside))
        full = pick(part_ref, slice(None)) + dot3(operator, halves(jnp.concatenate(halo, axis=1)))
        edge_ref[0] = full[:span, :width] - full[span:, width:]
        edge_ref[1] = full[:span, width:] + full[span:, :width]
        rows = pl.ds(pl.multiple_of(jnp.where(up, 0, chunks * width - span), 8), span)
        copy = pltpu.make_async_copy(edge_ref, out_hbm.at[:, rows, :], sems.at[1])
        copy.start()
        copy.wait()

    image_copy.wait()


def around(rcv, freq, sign):
    pairs = []
    for at in range(rcv):
        for slot in range(freq):
            target = at + (sign if slot % 2 == 0 else -sign)
            to_slot = slot
            if not 0 <= target < rcv:
                target, to_slot = at, slot ^ 1
            pairs.append((at * freq + slot, target * freq + to_slot))
    return pairs


def between(src, freq):
    pairs = []
    for at in range(src):
        target = at - 1 if at % 2 == 0 else at + 1
        for slot in range(freq):
            ends = not 0 <= target < src
            pairs.append((at * freq + slot, at * freq + (slot ^ 1) if ends else target * freq + slot))
    return pairs


def far_pairs(freq):
    pairs = []
    for slot in range(0, freq, 2):
        moves = {
            (1, 0): (1, 1), (1, 1): (3, 0), (3, 0): (1, 0),
            (0, 0): (2, 0), (2, 0): (2, 1), (2, 1): (0, 0),
            (0, 1): (3, 1), (3, 1): (0, 1),
        }
        for (at, side), (to, to_side) in sorted(moves.items()):
            pairs.append((at * freq + slot + side, to * freq + slot + to_side))
    return pairs


def body(wavefield, op_table, vel_index, interp_index, interp_weight, freq_perm):
    rows, width = wavefield.shape[2], wavefield.shape[3]
    n_src, n_rcv, n_freq = (lax.axis_size(axis) for axis in ("src", "rcv", "freq"))
    lateral = width * n_rcv
    rim = SUBSTEPS * (op_table.shape[2] // 2)
    edge = -(-(rim + 1) // 8) * 8
    half = width // 2
    chunks = rows // width
    wave = wavefield.reshape(2 * rows, width)

    vmem = pl.BlockSpec(memory_space=pltpu.VMEM)
    anywhere = pl.BlockSpec(memory_space=pltpu.HBM)
    params = pltpu.CompilerParams(vmem_limit_bytes=VMEM_LIMIT)
    cost = pl.CostEstimate(flops=6 * 2**28, bytes_accessed=2**20, transcendentals=0)

    small = max(vel_index.shape[0], interp_index.shape[0], width)
    rows_of = lambda a: jnp.pad(a.astype(F32), ((0, 0), (0, small - a.shape[1])))
    tables = [
        jnp.concatenate(
            [rows_of(vel_index.reshape(1, -1)), jnp.pad(freq_perm, (0, small - 1)).astype(F32).reshape(1, -1), rows_of(interp_index.T), rows_of(interp_weight.T)]
        ),
        op_table.transpose(2, 0, 1),
    ]
    _, groups = groups_of(2 * rows, width, rim)
    packed = jax.ShapeDtypeStruct((groups[0][1], width), F32)
    first, second = pl.pallas_call(
        functools.partial(pack_kernel, rim),
        out_shape=[packed, packed],
        in_specs=[vmem],
        out_specs=[vmem] * 2,
        compiler_params=params,
        name="pack",
    )(wave)
    first = lax.ppermute(first, ("rcv", "freq"), around(n_rcv, n_freq, -1))
    second = lax.ppermute(second, ("rcv", "freq"), around(n_rcv, n_freq, 1))

    square = (2 * width, 2 * width)
    rcv_full, rcv_high, rcv_low, found = pl.pallas_call(
        functools.partial(rcv_operator_kernel, lateral),
        out_shape=[
            jax.ShapeDtypeStruct(square, F32),
            jax.ShapeDtypeStruct(square, BF16),
            jax.ShapeDtypeStruct(square, BF16),
            jax.ShapeDtypeStruct((2, (chunks + 1) * 2 * width // TILE, width), F32),
        ],
        in_specs=[vmem] * 2,
        out_specs=[vmem] * 4,
        scratch_shapes=[pltpu.VMEM((2, width, op_table.shape[1]), F32), pltpu.VMEM((2,) + square, F32)],
        compiler_params=params,
        cost_estimate=cost,
        name="rcv_operator",
    )(*tables)
    field, one, two, image = pl.pallas_call(
        functools.partial(receiver_kernel, rim),
        out_shape=[
            jax.ShapeDtypeStruct((2, rows, width), F32),
            jax.ShapeDtypeStruct((2, edge, width), F32),
            jax.ShapeDtypeStruct((2, edge, width), F32),
            jax.ShapeDtypeStruct((1, width), F32),
        ],
        in_specs=[vmem] * 6,
        out_specs=[vmem] * 4,
        compiler_params=params,
        name="receivers",
    )(wave, first, second, rcv_full, rcv_high, rcv_low)

    if n_freq == 2:
        other = lax.ppermute(one, "freq", [(0, 1), (1, 0)])
        image = image + jnp.where(lax.axis_index("src") % 2 == 0, other[0, :1], other[0, edge - 1 :])
    else:
        image = lax.psum(image, "freq")
    one = lax.ppermute(one, "src", [(i, i + 1 if i % 2 == 0 else i - 1) for i in range(n_src)])
    up = lax.axis_index("src") % 2 == 0
    if n_src == 4:
        far = lax.ppermute(image, ("src", "freq"), far_pairs(n_freq))
        two = lax.dynamic_update_slice(two, image[None], (0, jnp.where(up, edge - 1, 0), 0))
    two = lax.ppermute(two, ("src", "freq"), between(n_src, n_freq))
    one, found = lax.optimization_barrier((one, found))
    src_high, src_low = pl.pallas_call(
        functools.partial(src_operator_kernel, lateral, op_table.shape[2]),
        out_shape=[jax.ShapeDtypeStruct((chunks,) + square, BF16)] * 2,
        in_specs=[vmem],
        out_specs=[vmem] * 2,
        scratch_shapes=[pltpu.VMEM((2,) + square, F32)],
        compiler_params=params,
        cost_estimate=pl.CostEstimate(flops=2**20, bytes_accessed=2**10, transcendentals=0),
        name="src_operator",
    )(found)
    if n_src == 4:
        at, slot = lax.axis_index("src"), lax.axis_index("freq")
        from_one = jnp.where(up, one[0, edge - 1 :], one[0, :1])
        other = jnp.logical_or(jnp.logical_and(at == 1, slot == 1), jnp.logical_and(at == 2, slot == 1))
        from_far = jnp.where(jnp.logical_or(other, slot > 1), 0.0, far)
        near, src_high = lax.optimization_barrier((from_one + from_far, src_high))
        if n_freq == 2:
            images = [image, near, lax.ppermute(near, "freq", [(0, 1), (1, 0)])]
        else:
            images = [image, lax.psum(near, "freq")]
    else:
        images = [lax.psum(image, "src")]
    sunk, parts = pl.pallas_call(
        inner_kernel,
        out_shape=[jax.ShapeDtypeStruct((2, rows, width), F32), jax.ShapeDtypeStruct((chunks,) + square, F32)],
        in_specs=[vmem] * 4,
        out_specs=[vmem] * 2,
        compiler_params=params,
        cost_estimate=cost,
        name="inner",
    )(field, one, src_high, src_low)
    span = -(-edge // 16) * 16
    anywhere = pl.BlockSpec(memory_space=pl.ANY)
    sunk, image = pl.pallas_call(
        source_kernel,
        out_shape=[jax.ShapeDtypeStruct((2, rows, width), F32), jax.ShapeDtypeStruct((1, width), F32)],
        in_specs=[anywhere] + [vmem] * (4 + len(images)),
        out_specs=[anywhere] * 2,
        scratch_shapes=[
            pltpu.VMEM((2, span, width), F32),
            pltpu.VMEM((1, width), F32),
            pltpu.SemaphoreType.DMA((2,)),
        ],
        input_output_aliases={0: 0},
        compiler_params=params,
        name="sources",
    )(sunk, parts, two, src_high, src_low, *images)
    return sunk.reshape(wavefield.shape), image.reshape(width)


def solution(mesh):
    in_specs = (P(None, "freq", "src", "rcv"), P(), P(), P(), P(), P("freq"))
    out_specs = (P(None, "freq", "src", "rcv"), P("rcv"))
    return jax.shard_map(body, mesh=mesh, in_specs=in_specs, out_specs=out_specs, check_vma=False)
```

```python
import functools

import jax
import jax.numpy as jnp
from jax import lax
from jax.experimental import pallas as pl
from jax.experimental.pallas import tpu as pltpu
from jax.sharding import PartitionSpec as P

SUBSTEPS = 4
TILE = 16
VMEM_LIMIT = 32 * 1024 * 1024
F32 = jnp.float32
BF16 = jnp.bfloat16


def halves(value):
    high = value.astype(BF16)
    low = (value - high.astype(F32)).astype(BF16)
    return high, low


def dot(left, right):
    return jnp.dot(left, right, preferred_element_type=F32)


def dot3(left, right):
    left_high, left_low = left
    right_high, right_low = right
    return dot(left_high, right_high) + (dot(left_high, right_low) + dot(left_low, right_high))


def complex_product(left, right):
    first = dot3(halves(left[0]), halves(right[0]))
    second = dot3(halves(left[1]), halves(right[1]))
    third = dot3(halves(left[0] + left[1]), halves(right[0] + right[1]))
    return first - second, third - first - second


def tile_taps(lateral_tiles, starts, window, small_ref, table_ref, table):
    count = window // TILE
    slots = (small_ref.shape[0] - 2) // 2
    tiles = velocities = small_ref.shape[1]
    entries, taps = table_ref.shape[2], table_ref.shape[0]
    place = lax.broadcasted_iota(jnp.int32, (count, tiles), 0)
    place = place - jnp.where(place >= count - count // 4, count, 0)
    tile = jnp.concatenate([start // TILE + place for start in starts], axis=0)
    lane = lax.broadcasted_iota(jnp.int32, tile.shape, 1)
    velocity = jnp.sum(jnp.where(lane == tile, small_ref[:1], 0.0), axis=1, keepdims=True)
    inside = jnp.logical_and(tile[:, :1] >= 0, tile[:, :1] < lateral_tiles).astype(F32)
    chosen = lax.broadcasted_iota(jnp.int32, (slots, velocities), 0).astype(F32) == small_ref[1:2, :1]
    index = jnp.sum(jnp.where(chosen, small_ref[2 : 2 + slots], 0.0), axis=0, keepdims=True)
    weight = jnp.sum(jnp.where(chosen, small_ref[2 + slots :], 0.0), axis=0, keepdims=True)
    rows = tile.shape[0]
    hit = lax.broadcasted_iota(jnp.int32, (rows, velocities), 1).astype(F32) == velocity
    index = jnp.sum(jnp.where(hit, index, 0.0), axis=1, keepdims=True)
    weight = jnp.sum(jnp.where(hit, weight, 0.0), axis=1, keepdims=True)
    entry = lax.broadcasted_iota(jnp.int32, (rows, entries), 1).astype(F32)
    mix = jnp.where(entry == index, 1.0 - weight, 0.0) + jnp.where(entry == index + 1.0, weight, 0.0)
    mix = mix * inside
    table[...] = jnp.zeros_like(table)
    found = []
    for part in range(2):
        table[part, :taps, :] = table_ref[:, part, :]
        found.append(
            lax.dot_general(
                mix, table[part], (((1,), (1,)), ((), ())), precision=lax.Precision.HIGHEST, preferred_element_type=F32
            )
        )
    return found


def fill_band(found, first, taps, band):
    window = band.shape[1]
    for position in range(window // TILE):
        shift = (position * TILE - taps // 2) % window
        for part in range(2):
            row = found[part][first + position : first + position + 1]
            spread = jnp.broadcast_to(row, (TILE, row.shape[1]))
            slanted = pltpu.roll(spread, 0, 1, stride=1, stride_axis=0)
            wide = jnp.concatenate([slanted, jnp.zeros((TILE, window - slanted.shape[1]), F32)], axis=1)
            band[part, pl.ds(position * TILE, TILE), :] = pltpu.roll(wide, shift, 1)


def four_substeps(start, lateral, once):
    window = once[0].shape[0]
    width = window // 2
    twice = complex_product(once, once)
    four = complex_product((twice[0][:width], twice[1][:width]), twice)
    place = lax.broadcasted_iota(jnp.int32, (width, window), 1)
    cell = start + jnp.where(place < window - width // 2, place, place - window)
    inside = jnp.logical_and(cell >= 0, cell < lateral)
    return jnp.where(inside, four[0], 0.0), jnp.where(inside, four[1], 0.0)


def groups_of(rows, width, rim):
    count = width // rim
    step = -(-rows // (8 * count)) * 8
    return width // count, [(low, min(low + step, rows)) for low in range(0, rows, step)]


def pack_kernel(rim, wave_ref, one_ref, two_ref):
    rows, width = wave_ref.shape
    span, groups = groups_of(rows, width, rim)
    odd = lax.axis_index("freq") % 2 == 1
    lane = lax.broadcasted_iota(jnp.int32, one_ref.shape, 1)
    packed = []
    for sign in (1, -1):
        message = wave_ref[: groups[0][1]]
        for index, (low, high) in enumerate(groups[1:], 1):
            count = high - low
            place = lane[:count] if sign == 1 else width - 1 - lane[:count]
            moved = pltpu.roll(wave_ref[low:high], sign * index * span % width, 1)
            top = jnp.where(place // span == index, moved, message[:count])
            message = top if count == message.shape[0] else jnp.concatenate([top, message[count:]], axis=0)
        packed.append(message)
    one_ref[...] = jnp.where(odd, packed[1], packed[0])
    two_ref[...] = jnp.where(odd, packed[0], packed[1])


def rcv_operator_kernel(
    lateral, small_ref, table_ref, full_ref, high_ref, low_ref, found_ref, table, band
):
    width = full_ref.shape[1] // 2
    taps, window = table_ref.shape[0], 2 * width
    chunks = found_ref.shape[1] * TILE // window - 1
    starts = [lax.axis_index("rcv") * width]
    starts += [(lax.axis_index("src") * chunks + chunk) * width for chunk in range(chunks)]
    found = tile_taps(lateral // TILE, starts, window, small_ref, table_ref, table)
    fill_band(found, 0, taps, band)
    for part in range(2):
        found_ref[part] = found[part]
    real, imag = four_substeps(starts[0], lateral, (band[0], band[1]))
    turned = jnp.concatenate([real.T, imag.T], axis=1)
    full_ref[...] = turned
    high_ref[...], low_ref[...] = halves(turned)


def src_operator_kernel(lateral, taps, found_ref, high_ref, low_ref, band):
    chunks, width = high_ref.shape[0], high_ref.shape[2] // 2
    found = (found_ref[0], found_ref[1])
    for chunk in range(chunks):
        start = (lax.axis_index("src") * chunks + chunk) * width
        fill_band(found, (chunk + 1) * 2 * width // TILE, taps, band)
        real, imag = four_substeps(start, lateral, (band[0], band[1]))
        high_ref[chunk], low_ref[chunk] = halves(jnp.concatenate([real, imag], axis=0))


def receiver_kernel(rim, wave_ref, first_ref, second_ref, full_ref, high_ref, low_ref, sunk_ref, one_ref, two_ref, image_ref):
    rows, width = sunk_ref.shape[1], sunk_ref.shape[2]
    half = width // 2
    span, groups = groups_of(2 * rows, width, rim)
    odd = lax.axis_index("freq") % 2 == 1
    before = jnp.where(odd, first_ref[...], second_ref[...])
    after = jnp.where(odd, second_ref[...], first_ref[...])
    halos = []
    for index, (low, high) in enumerate(groups):
        left, right = after[: high - low], before[: high - low]
        if index:
            left = pltpu.roll(left, -index * span % width, 1)
            right = pltpu.roll(right, index * span % width, 1)
        lane = lax.broadcasted_iota(jnp.int32, left.shape, 1)
        halos.append(jnp.where(lane < half, left, right))
    extended = jnp.concatenate([wave_ref[...], jnp.concatenate(halos, axis=0)], axis=1)
    full = dot3(halves(extended), (high_ref[...], low_ref[...]))
    real = full[:rows, :width] - full[rows:, width:]
    imag = full[:rows, width:] + full[rows:, :width]
    sunk_ref[0] = real
    sunk_ref[1] = imag
    chunks = rows // width
    ahead = lax.axis_index("src") * chunks - lax.axis_index("rcv")
    line = lax.broadcasted_iota(jnp.int32, (width, 2 * width), 0)
    image = jnp.zeros((1, width), F32)
    for chunk in range(chunks):
        away = ahead + chunk
        beside = jnp.logical_or(
            jnp.logical_and(away == 1, line < half), jnp.logical_and(away == -1, line >= half)
        )
        weights = jnp.where(away == 0, full_ref[:width], jnp.where(beside, full_ref[width:], 0.0))
        piece = slice(chunk * width, (chunk + 1) * width)
        terms = weights[:, :width] * real[piece] - weights[:, width:] * imag[piece]
        image = image + jnp.sum(terms, axis=0, keepdims=True)
    image_ref[...] = image
    edge = one_ref.shape[1]
    row = lax.broadcasted_iota(jnp.int32, (edge, width), 0)
    head = (jnp.where(row == edge - 1, image, real[:edge]), imag[:edge])
    tail = (jnp.where(row == 0, image, real[rows - edge :]), imag[rows - edge :])
    up = lax.axis_index("src") % 2 == 0
    for part in range(2):
        one_ref[part] = jnp.where(up, tail[part], head[part])
        two_ref[part] = jnp.where(up, head[part], tail[part])


def inner_kernel(field_ref, one_ref, high_ref, low_ref, out_ref, part_ref):
    rows, width = field_ref.shape[1], field_ref.shape[2]
    half = width // 2
    chunks = rows // width
    up = lax.axis_index("src") % 2 == 0
    gap = jnp.zeros((half - one_ref.shape[1], width), F32)
    for chunk in range(chunks):
        low, high = chunk * width, (chunk + 1) * width
        extended = []
        for part in range(2):
            if chunk + 1 < chunks:
                after = field_ref[part, high : high + half]
            else:
                after = jnp.concatenate([jnp.where(up, one_ref[part], 0.0), gap], axis=0)
            if chunk > 0:
                before = field_ref[part, low - half : low]
            else:
                before = jnp.concatenate([gap, jnp.where(up, 0.0, one_ref[part])], axis=0)
            extended.append(jnp.concatenate([field_ref[part, low:high], after, before], axis=0))
        full = dot3((high_ref[chunk], low_ref[chunk]), halves(jnp.concatenate(extended, axis=1)))
        part_ref[chunk] = full
        out_ref[0, low:high] = full[:width, :width] - full[width:, width:]
        out_ref[1, low:high] = full[:width, width:] + full[width:, :width]


def source_kernel(sunk_hbm, part_ref, two_ref, high_ref, low_ref, *rest):
    *image_refs, out_hbm, image_hbm, edge_ref, image_ref, sems = rest
    del sunk_hbm
    chunks, width = part_ref.shape[0], two_ref.shape[2]
    half, edge, span = width // 2, two_ref.shape[1], edge_ref.shape[1]
    at = lax.axis_index("src")
    up = at % 2 == 0
    inner = jnp.logical_and(at > 0, at < lax.axis_size("src") - 1)
    image = functools.reduce(jnp.add, [ref[...] for ref in image_refs])
    if len(image_refs) > 1:
        from_two = jnp.where(up, two_ref[0, :1], two_ref[0, edge - 1 :])
        image = image + jnp.where(inner, from_two, 0.0)
    image_ref[...] = image
    image_copy = pltpu.make_async_copy(image_ref, image_hbm, sems.at[0])
    image_copy.start()

    @pl.when(inner)
    def _():
        none = jnp.zeros((half, width), F32)
        gap = none[: half - edge]
        first, last = slice(0, span), slice(width - span, width)

        def pick(ref, columns):
            chosen = [
                jnp.concatenate([ref[chunk, :width, columns][rows], ref[chunk, width:, columns][rows]], axis=0)
                for chunk, rows in ((0, first), (chunks - 1, last))
            ]
            return jnp.where(up, *chosen)

        halo = []
        for part in range(2):
            before = jnp.concatenate([none, gap, two_ref[part]], axis=0)
            after = jnp.concatenate([two_ref[part], gap, none], axis=0)
            halo.append(jnp.where(up, before, after))
        beside = slice(width, 2 * width)
        operator = (pick(high_ref, beside), pick(low_ref, beside))
        full = pick(part_ref, slice(None)) + dot3(operator, halves(jnp.concatenate(halo, axis=1)))
        edge_ref[0] = full[:span, :width] - full[span:, width:]
        edge_ref[1] = full[:span, width:] + full[span:, :width]
        rows = pl.ds(pl.multiple_of(jnp.where(up, 0, chunks * width - span), 8), span)
        copy = pltpu.make_async_copy(edge_ref, out_hbm.at[:, rows, :], sems.at[1])
        copy.start()
        copy.wait()

    image_copy.wait()


def around(rcv, freq, sign):
    pairs = []
    for at in range(rcv):
        for slot in range(freq):
            target = at + (sign if slot % 2 == 0 else -sign)
            to_slot = slot
            if not 0 <= target < rcv:
                target, to_slot = at, slot ^ 1
            pairs.append((at * freq + slot, target * freq + to_slot))
    return pairs


def between(src, freq):
    pairs = []
    for at in range(src):
        target = at - 1 if at % 2 == 0 else at + 1
        for slot in range(freq):
            ends = not 0 <= target < src
            pairs.append((at * freq + slot, at * freq + (slot ^ 1) if ends else target * freq + slot))
    return pairs


def far_pairs(freq):
    pairs = []
    for slot in range(0, freq, 2):
        moves = {
            (1, 0): (1, 1), (1, 1): (3, 0), (3, 0): (1, 0),
            (0, 0): (2, 0), (2, 0): (2, 1), (2, 1): (0, 0),
            (0, 1): (3, 1), (3, 1): (0, 1),
        }
        for (at, side), (to, to_side) in sorted(moves.items()):
            pairs.append((at * freq + slot + side, to * freq + slot + to_side))
    return pairs


def body(wavefield, op_table, vel_index, interp_index, interp_weight, freq_perm):
    rows, width = wavefield.shape[2], wavefield.shape[3]
    n_src, n_rcv, n_freq = (lax.axis_size(axis) for axis in ("src", "rcv", "freq"))
    lateral = width * n_rcv
    rim = SUBSTEPS * (op_table.shape[2] // 2)
    edge = -(-(rim + 1) // 8) * 8
    half = width // 2
    chunks = rows // width
    wave = wavefield.reshape(2 * rows, width)

    vmem = pl.BlockSpec(memory_space=pltpu.VMEM)
    anywhere = pl.BlockSpec(memory_space=pltpu.HBM)
    params = pltpu.CompilerParams(vmem_limit_bytes=VMEM_LIMIT)
    cost = pl.CostEstimate(flops=6 * 2**28, bytes_accessed=2**20, transcendentals=0)

    small = max(vel_index.shape[0], interp_index.shape[0], width)
    rows_of = lambda a: jnp.pad(a.astype(F32), ((0, 0), (0, small - a.shape[1])))
    tables = [
        jnp.concatenate(
            [rows_of(vel_index.reshape(1, -1)), jnp.pad(freq_perm, (0, small - 1)).astype(F32).reshape(1, -1), rows_of(interp_index.T), rows_of(interp_weight.T)]
        ),
        op_table.transpose(2, 0, 1),
    ]
    _, groups = groups_of(2 * rows, width, rim)
    packed = jax.ShapeDtypeStruct((groups[0][1], width), F32)
    first, second = pl.pallas_call(
        functools.partial(pack_kernel, rim),
        out_shape=[packed, packed],
        in_specs=[vmem],
        out_specs=[vmem] * 2,
        compiler_params=params,
        name="pack",
    )(wave)
    first = lax.ppermute(first, ("rcv", "freq"), around(n_rcv, n_freq, -1))
    second = lax.ppermute(second, ("rcv", "freq"), around(n_rcv, n_freq, 1))

    square = (2 * width, 2 * width)
    rcv_full, rcv_high, rcv_low, found = pl.pallas_call(
        functools.partial(rcv_operator_kernel, lateral),
        out_shape=[
            jax.ShapeDtypeStruct(square, F32),
            jax.ShapeDtypeStruct(square, BF16),
            jax.ShapeDtypeStruct(square, BF16),
            jax.ShapeDtypeStruct((2, (chunks + 1) * 2 * width // TILE, width), F32),
        ],
        in_specs=[vmem] * 2,
        out_specs=[vmem] * 4,
        scratch_shapes=[pltpu.VMEM((2, width, op_table.shape[1]), F32), pltpu.VMEM((2,) + square, F32)],
        compiler_params=params,
        cost_estimate=cost,
        name="rcv_operator",
    )(*tables)
    field, one, two, image = pl.pallas_call(
        functools.partial(receiver_kernel, rim),
        out_shape=[
            jax.ShapeDtypeStruct((2, rows, width), F32),
            jax.ShapeDtypeStruct((2, edge, width), F32),
            jax.ShapeDtypeStruct((2, edge, width), F32),
            jax.ShapeDtypeStruct((1, width), F32),
        ],
        in_specs=[vmem] * 6,
        out_specs=[vmem] * 4,
        compiler_params=params,
        name="receivers",
    )(wave, first, second, rcv_full, rcv_high, rcv_low)

    if n_freq == 2:
        other = lax.ppermute(one, "freq", [(0, 1), (1, 0)])
        image = image + jnp.where(lax.axis_index("src") % 2 == 0, other[0, :1], other[0, edge - 1 :])
    else:
        image = lax.psum(image, "freq")
    one = lax.ppermute(one, "src", [(i, i + 1 if i % 2 == 0 else i - 1) for i in range(n_src)])
    up = lax.axis_index("src") % 2 == 0
    if n_src == 4:
        far = lax.ppermute(image, ("src", "freq"), far_pairs(n_freq))
        two = lax.dynamic_update_slice(two, image[None], (0, jnp.where(up, edge - 1, 0), 0))
    two, found = lax.optimization_barrier((two, found))
    two = lax.ppermute(two, ("src", "freq"), between(n_src, n_freq))
    src_high, src_low = pl.pallas_call(
        functools.partial(src_operator_kernel, lateral, op_table.shape[2]),
        out_shape=[jax.ShapeDtypeStruct((chunks,) + square, BF16)] * 2,
        in_specs=[vmem],
        out_specs=[vmem] * 2,
        scratch_shapes=[pltpu.VMEM((2,) + square, F32)],
        compiler_params=params,
        cost_estimate=pl.CostEstimate(flops=2**20, bytes_accessed=2**10, transcendentals=0),
        name="src_operator",
    )(found)
    if n_src == 4:
        at, slot = lax.axis_index("src"), lax.axis_index("freq")
        from_one = jnp.where(up, one[0, edge - 1 :], one[0, :1])
        other = jnp.logical_or(jnp.logical_and(at == 1, slot == 1), jnp.logical_and(at == 2, slot == 1))
        from_far = jnp.where(jnp.logical_or(other, slot > 1), 0.0, far)
        near, src_high = lax.optimization_barrier((from_one + from_far, src_high))
        if n_freq == 2:
            images = [image, near, lax.ppermute(near, "freq", [(0, 1), (1, 0)])]
        else:
            images = [image, lax.psum(near, "freq")]
    else:
        images = [lax.psum(image, "src")]
    sunk, parts = pl.pallas_call(
        inner_kernel,
        out_shape=[jax.ShapeDtypeStruct((2, rows, width), F32), jax.ShapeDtypeStruct((chunks,) + square, F32)],
        in_specs=[vmem] * 4,
        out_specs=[vmem] * 2,
        compiler_params=params,
        cost_estimate=cost,
        name="inner",
    )(field, one, src_high, src_low)
    span = -(-edge // 16) * 16
    anywhere = pl.BlockSpec(memory_space=pl.ANY)
    sunk, image = pl.pallas_call(
        source_kernel,
        out_shape=[jax.ShapeDtypeStruct((2, rows, width), F32), jax.ShapeDtypeStruct((1, width), F32)],
        in_specs=[anywhere] + [vmem] * (4 + len(images)),
        out_specs=[anywhere] * 2,
        scratch_shapes=[
            pltpu.VMEM((2, span, width), F32),
            pltpu.VMEM((1, width), F32),
            pltpu.SemaphoreType.DMA((2,)),
        ],
        input_output_aliases={0: 0},
        compiler_params=params,
        name="sources",
    )(sunk, parts, two, src_high, src_low, *images)
    return sunk.reshape(wavefield.shape), image.reshape(width)


def solution(mesh):
    in_specs = (P(None, "freq", "src", "rcv"), P(), P(), P(), P(), P("freq"))
    out_specs = (P(None, "freq", "src", "rcv"), P("rcv"))
    return jax.shard_map(body, mesh=mesh, in_specs=in_specs, out_specs=out_specs, check_vma=False)
```

```python
import functools

import jax
import jax.numpy as jnp
from jax import lax
from jax.experimental import pallas as pl
from jax.experimental.pallas import tpu as pltpu
from jax.sharding import PartitionSpec as P

SUBSTEPS = 4
TILE = 16
VMEM_LIMIT = 32 * 1024 * 1024
F32 = jnp.float32
BF16 = jnp.bfloat16


def halves(value):
    high = value.astype(BF16)
    low = (value - high.astype(F32)).astype(BF16)
    return high, low


def dot(left, right):
    return jnp.dot(left, right, preferred_element_type=F32)


def dot3(left, right):
    left_high, left_low = left
    right_high, right_low = right
    return dot(left_high, right_high) + (dot(left_high, right_low) + dot(left_low, right_high))


def complex_product(left, right):
    first = dot3(halves(left[0]), halves(right[0]))
    second = dot3(halves(left[1]), halves(right[1]))
    third = dot3(halves(left[0] + left[1]), halves(right[0] + right[1]))
    return first - second, third - first - second


def tile_taps(lateral_tiles, starts, window, small_ref, table_ref, table):
    count = window // TILE
    slots = (small_ref.shape[0] - 2) // 2
    tiles = velocities = small_ref.shape[1]
    entries, taps = table_ref.shape[2], table_ref.shape[0]
    place = lax.broadcasted_iota(jnp.int32, (count, tiles), 0)
    place = place - jnp.where(place >= count - count // 4, count, 0)
    tile = jnp.concatenate([start // TILE + place for start in starts], axis=0)
    lane = lax.broadcasted_iota(jnp.int32, tile.shape, 1)
    velocity = jnp.sum(jnp.where(lane == tile, small_ref[:1], 0.0), axis=1, keepdims=True)
    inside = jnp.logical_and(tile[:, :1] >= 0, tile[:, :1] < lateral_tiles).astype(F32)
    chosen = lax.broadcasted_iota(jnp.int32, (slots, velocities), 0).astype(F32) == small_ref[1:2, :1]
    index = jnp.sum(jnp.where(chosen, small_ref[2 : 2 + slots], 0.0), axis=0, keepdims=True)
    weight = jnp.sum(jnp.where(chosen, small_ref[2 + slots :], 0.0), axis=0, keepdims=True)
    rows = tile.shape[0]
    hit = lax.broadcasted_iota(jnp.int32, (rows, velocities), 1).astype(F32) == velocity
    index = jnp.sum(jnp.where(hit, index, 0.0), axis=1, keepdims=True)
    weight = jnp.sum(jnp.where(hit, weight, 0.0), axis=1, keepdims=True)
    entry = lax.broadcasted_iota(jnp.int32, (rows, entries), 1).astype(F32)
    mix = jnp.where(entry == index, 1.0 - weight, 0.0) + jnp.where(entry == index + 1.0, weight, 0.0)
    mix = mix * inside
    table[...] = jnp.zeros_like(table)
    found = []
    for part in range(2):
        table[part, :taps, :] = table_ref[:, part, :]
        found.append(
            lax.dot_general(
                mix, table[part], (((1,), (1,)), ((), ())), precision=lax.Precision.HIGHEST, preferred_element_type=F32
            )
        )
    return found


def fill_band(found, first, taps, band):
    window = band.shape[1]
    for position in range(window // TILE):
        shift = (position * TILE - taps // 2) % window
        for part in range(2):
            row = found[part][first + position : first + position + 1]
            spread = jnp.broadcast_to(row, (TILE, row.shape[1]))
            slanted = pltpu.roll(spread, 0, 1, stride=1, stride_axis=0)
            wide = jnp.concatenate([slanted, jnp.zeros((TILE, window - slanted.shape[1]), F32)], axis=1)
            band[part, pl.ds(position * TILE, TILE), :] = pltpu.roll(wide, shift, 1)


def four_substeps(start, lateral, once):
    window = once[0].shape[0]
    width = window // 2
    twice = complex_product(once, once)
    four = complex_product((twice[0][:width], twice[1][:width]), twice)
    place = lax.broadcasted_iota(jnp.int32, (width, window), 1)
    cell = start + jnp.where(place < window - width // 2, place, place - window)
    inside = jnp.logical_and(cell >= 0, cell < lateral)
    return jnp.where(inside, four[0], 0.0), jnp.where(inside, four[1], 0.0)


def groups_of(rows, width, rim):
    count = width // rim
    step = -(-rows // (8 * count)) * 8
    return width // count, [(low, min(low + step, rows)) for low in range(0, rows, step)]


def pack_kernel(rim, wave_ref, one_ref, two_ref):
    rows, width = wave_ref.shape
    span, groups = groups_of(rows, width, rim)
    odd = lax.axis_index("freq") % 2 == 1
    lane = lax.broadcasted_iota(jnp.int32, one_ref.shape, 1)
    packed = []
    for sign in (1, -1):
        message = wave_ref[: groups[0][1]]
        for index, (low, high) in enumerate(groups[1:], 1):
            count = high - low
            place = lane[:count] if sign == 1 else width - 1 - lane[:count]
            moved = pltpu.roll(wave_ref[low:high], sign * index * span % width, 1)
            top = jnp.where(place // span == index, moved, message[:count])
            message = top if count == message.shape[0] else jnp.concatenate([top, message[count:]], axis=0)
        packed.append(message)
    one_ref[...] = jnp.where(odd, packed[1], packed[0])
    two_ref[...] = jnp.where(odd, packed[0], packed[1])


def rcv_operator_kernel(
    lateral, small_ref, table_ref, full_ref, high_ref, low_ref, found_ref, table, band
):
    width = full_ref.shape[1] // 2
    taps, window = table_ref.shape[0], 2 * width
    chunks = found_ref.shape[1] * TILE // window - 1
    starts = [lax.axis_index("rcv") * width]
    starts += [(lax.axis_index("src") * chunks + chunk) * width for chunk in range(chunks)]
    found = tile_taps(lateral // TILE, starts, window, small_ref, table_ref, table)
    fill_band(found, 0, taps, band)
    for part in range(2):
        found_ref[part] = found[part]
    real, imag = four_substeps(starts[0], lateral, (band[0], band[1]))
    turned = jnp.concatenate([real.T, imag.T], axis=1)
    full_ref[...] = turned
    high_ref[...], low_ref[...] = halves(turned)


def src_operator_kernel(lateral, taps, found_ref, high_ref, low_ref, band):
    chunks, width = high_ref.shape[0], high_ref.shape[2] // 2
    found = (found_ref[0], found_ref[1])
    for chunk in range(chunks):
        start = (lax.axis_index("src") * chunks + chunk) * width
        fill_band(found, (chunk + 1) * 2 * width // TILE, taps, band)
        real, imag = four_substeps(start, lateral, (band[0], band[1]))
        high_ref[chunk], low_ref[chunk] = halves(jnp.concatenate([real, imag], axis=0))


def receiver_kernel(rim, wave_ref, first_ref, second_ref, full_ref, high_ref, low_ref, sunk_ref, one_ref, two_ref, image_ref):
    rows, width = sunk_ref.shape[1], sunk_ref.shape[2]
    half = width // 2
    span, groups = groups_of(2 * rows, width, rim)
    odd = lax.axis_index("freq") % 2 == 1
    before = jnp.where(odd, first_ref[...], second_ref[...])
    after = jnp.where(odd, second_ref[...], first_ref[...])
    halos = []
    for index, (low, high) in enumerate(groups):
        left, right = after[: high - low], before[: high - low]
        if index:
            left = pltpu.roll(left, -index * span % width, 1)
            right = pltpu.roll(right, index * span % width, 1)
        lane = lax.broadcasted_iota(jnp.int32, left.shape, 1)
        halos.append(jnp.where(lane < half, left, right))
    extended = jnp.concatenate([wave_ref[...], jnp.concatenate(halos, axis=0)], axis=1)
    full = dot3(halves(extended), (high_ref[...], low_ref[...]))
    real = full[:rows, :width] - full[rows:, width:]
    imag = full[:rows, width:] + full[rows:, :width]
    sunk_ref[0] = real
    sunk_ref[1] = imag
    chunks = rows // width
    ahead = lax.axis_index("src") * chunks - lax.axis_index("rcv")
    line = lax.broadcasted_iota(jnp.int32, (width, 2 * width), 0)
    image = jnp.zeros((1, width), F32)
    for chunk in range(chunks):
        away = ahead + chunk
        beside = jnp.logical_or(
            jnp.logical_and(away == 1, line < half), jnp.logical_and(away == -1, line >= half)
        )
        weights = jnp.where(away == 0, full_ref[:width], jnp.where(beside, full_ref[width:], 0.0))
        piece = slice(chunk * width, (chunk + 1) * width)
        terms = weights[:, :width] * real[piece] - weights[:, width:] * imag[piece]
        image = image + jnp.sum(terms, axis=0, keepdims=True)
    image_ref[...] = image
    edge = one_ref.shape[1]
    row = lax.broadcasted_iota(jnp.int32, (edge, width), 0)
    head = (jnp.where(row == edge - 1, image, real[:edge]), imag[:edge])
    tail = (jnp.where(row == 0, image, real[rows - edge :]), imag[rows - edge :])
    up = lax.axis_index("src") % 2 == 0
    for part in range(2):
        one_ref[part] = jnp.where(up, tail[part], head[part])
        two_ref[part] = jnp.where(up, head[part], tail[part])


def inner_kernel(field_ref, one_ref, high_ref, low_ref, out_ref, part_ref):
    inner = jnp.logical_and(lax.axis_index("src") > 0, lax.axis_index("src") < lax.axis_size("src") - 1)
    rows, width = field_ref.shape[1], field_ref.shape[2]
    half = width // 2
    chunks = rows // width
    up = lax.axis_index("src") % 2 == 0
    gap = jnp.zeros((half - one_ref.shape[1], width), F32)
    for chunk in range(chunks):
        low, high = chunk * width, (chunk + 1) * width
        extended = []
        for part in range(2):
            if chunk + 1 < chunks:
                after = field_ref[part, high : high + half]
            else:
                after = jnp.concatenate([jnp.where(up, one_ref[part], 0.0), gap], axis=0)
            if chunk > 0:
                before = field_ref[part, low - half : low]
            else:
                before = jnp.concatenate([gap, jnp.where(up, 0.0, one_ref[part])], axis=0)
            extended.append(jnp.concatenate([field_ref[part, low:high], after, before], axis=0))
        full = dot3((high_ref[chunk], low_ref[chunk]), halves(jnp.concatenate(extended, axis=1)))
        if chunk in (0, chunks - 1):

            @pl.when(inner)
            def _(chunk=chunk, full=full):
                part_ref[chunk] = full

        out_ref[0, low:high] = full[:width, :width] - full[width:, width:]
        out_ref[1, low:high] = full[:width, width:] + full[width:, :width]


def source_kernel(sunk_hbm, part_ref, two_ref, high_ref, low_ref, *rest):
    *image_refs, out_hbm, image_hbm, edge_ref, image_ref, sems = rest
    del sunk_hbm
    chunks, width = part_ref.shape[0], two_ref.shape[2]
    half, edge, span = width // 2, two_ref.shape[1], edge_ref.shape[1]
    at = lax.axis_index("src")
    up = at % 2 == 0
    inner = jnp.logical_and(at > 0, at < lax.axis_size("src") - 1)
    image = functools.reduce(jnp.add, [ref[...] for ref in image_refs])
    if len(image_refs) > 1:
        from_two = jnp.where(up, two_ref[0, :1], two_ref[0, edge - 1 :])
        image = image + jnp.where(inner, from_two, 0.0)
    image_ref[...] = image
    image_copy = pltpu.make_async_copy(image_ref, image_hbm, sems.at[0])
    image_copy.start()

    @pl.when(inner)
    def _():
        none = jnp.zeros((half, width), F32)
        gap = none[: half - edge]
        first, last = slice(0, span), slice(width - span, width)

        def pick(ref, columns):
            chosen = [
                jnp.concatenate([ref[chunk, :width, columns][rows], ref[chunk, width:, columns][rows]], axis=0)
                for chunk, rows in ((0, first), (chunks - 1, last))
            ]
            return jnp.where(up, *chosen)

        halo = []
        for part in range(2):
            before = jnp.concatenate([none, gap, two_ref[part]], axis=0)
            after = jnp.concatenate([two_ref[part], gap, none], axis=0)
            halo.append(jnp.where(up, before, after))
        beside = slice(width, 2 * width)
        operator = (pick(high_ref, beside), pick(low_ref, beside))
        full = pick(part_ref, slice(None)) + dot3(operator, halves(jnp.concatenate(halo, axis=1)))
        edge_ref[0] = full[:span, :width] - full[span:, width:]
        edge_ref[1] = full[:span, width:] + full[span:, :width]
        rows = pl.ds(pl.multiple_of(jnp.where(up, 0, chunks * width - span), 8), span)
        copy = pltpu.make_async_copy(edge_ref, out_hbm.at[:, rows, :], sems.at[1])
        copy.start()
        copy.wait()

    image_copy.wait()


def around(rcv, freq, sign):
    pairs = []
    for at in range(rcv):
        for slot in range(freq):
            target = at + (sign if slot % 2 == 0 else -sign)
            to_slot = slot
            if not 0 <= target < rcv:
                target, to_slot = at, slot ^ 1
            pairs.append((at * freq + slot, target * freq + to_slot))
    return pairs


def between(src, freq):
    pairs = []
    for at in range(src):
        target = at - 1 if at % 2 == 0 else at + 1
        for slot in range(freq):
            ends = not 0 <= target < src
            pairs.append((at * freq + slot, at * freq + (slot ^ 1) if ends else target * freq + slot))
    return pairs


def far_pairs(freq):
    pairs = []
    for slot in range(0, freq, 2):
        moves = {
            (1, 0): (1, 1), (1, 1): (3, 0), (3, 0): (1, 0),
            (0, 0): (2, 0), (2, 0): (2, 1), (2, 1): (0, 0),
            (0, 1): (3, 1), (3, 1): (0, 1),
        }
        for (at, side), (to, to_side) in sorted(moves.items()):
            pairs.append((at * freq + slot + side, to * freq + slot + to_side))
    return pairs


def body(wavefield, op_table, vel_index, interp_index, interp_weight, freq_perm):
    rows, width = wavefield.shape[2], wavefield.shape[3]
    n_src, n_rcv, n_freq = (lax.axis_size(axis) for axis in ("src", "rcv", "freq"))
    lateral = width * n_rcv
    rim = SUBSTEPS * (op_table.shape[2] // 2)
    edge = -(-(rim + 1) // 8) * 8
    half = width // 2
    chunks = rows // width
    wave = wavefield.reshape(2 * rows, width)

    vmem = pl.BlockSpec(memory_space=pltpu.VMEM)
    anywhere = pl.BlockSpec(memory_space=pltpu.HBM)
    params = pltpu.CompilerParams(vmem_limit_bytes=VMEM_LIMIT)
    cost = pl.CostEstimate(flops=6 * 2**28, bytes_accessed=2**20, transcendentals=0)

    small = max(vel_index.shape[0], interp_index.shape[0], width)
    rows_of = lambda a: jnp.pad(a.astype(F32), ((0, 0), (0, small - a.shape[1])))
    tables = [
        jnp.concatenate(
            [rows_of(vel_index.reshape(1, -1)), jnp.pad(freq_perm, (0, small - 1)).astype(F32).reshape(1, -1), rows_of(interp_index.T), rows_of(interp_weight.T)]
        ),
        op_table.transpose(2, 0, 1),
    ]
    _, groups = groups_of(2 * rows, width, rim)
    packed = jax.ShapeDtypeStruct((groups[0][1], width), F32)
    first, second = pl.pallas_call(
        functools.partial(pack_kernel, rim),
        out_shape=[packed, packed],
        in_specs=[vmem],
        out_specs=[vmem] * 2,
        compiler_params=params,
        name="pack",
    )(wave)
    first = lax.ppermute(first, ("rcv", "freq"), around(n_rcv, n_freq, -1))
    second = lax.ppermute(second, ("rcv", "freq"), around(n_rcv, n_freq, 1))

    square = (2 * width, 2 * width)
    rcv_full, rcv_high, rcv_low, found = pl.pallas_call(
        functools.partial(rcv_operator_kernel, lateral),
        out_shape=[
            jax.ShapeDtypeStruct(square, F32),
            jax.ShapeDtypeStruct(square, BF16),
            jax.ShapeDtypeStruct(square, BF16),
            jax.ShapeDtypeStruct((2, (chunks + 1) * 2 * width // TILE, width), F32),
        ],
        in_specs=[vmem] * 2,
        out_specs=[vmem] * 4,
        scratch_shapes=[pltpu.VMEM((2, width, op_table.shape[1]), F32), pltpu.VMEM((2,) + square, F32)],
        compiler_params=params,
        cost_estimate=cost,
        name="rcv_operator",
    )(*tables)
    field, one, two, image = pl.pallas_call(
        functools.partial(receiver_kernel, rim),
        out_shape=[
            jax.ShapeDtypeStruct((2, rows, width), F32),
            jax.ShapeDtypeStruct((2, edge, width), F32),
            jax.ShapeDtypeStruct((2, edge, width), F32),
            jax.ShapeDtypeStruct((1, width), F32),
        ],
        in_specs=[vmem] * 6,
        out_specs=[vmem] * 4,
        compiler_params=params,
        name="receivers",
    )(wave, first, second, rcv_full, rcv_high, rcv_low)

    if n_freq == 2:
        other = lax.ppermute(one, "freq", [(0, 1), (1, 0)])
        image = image + jnp.where(lax.axis_index("src") % 2 == 0, other[0, :1], other[0, edge - 1 :])
    else:
        image = lax.psum(image, "freq")
    one = lax.ppermute(one, "src", [(i, i + 1 if i % 2 == 0 else i - 1) for i in range(n_src)])
    up = lax.axis_index("src") % 2 == 0
    if n_src == 4:
        far = lax.ppermute(image, ("src", "freq"), far_pairs(n_freq))
        two = lax.dynamic_update_slice(two, image[None], (0, jnp.where(up, edge - 1, 0), 0))
    two, found = lax.optimization_barrier((two, found))
    two = lax.ppermute(two, ("src", "freq"), between(n_src, n_freq))
    src_high, src_low = pl.pallas_call(
        functools.partial(src_operator_kernel, lateral, op_table.shape[2]),
        out_shape=[jax.ShapeDtypeStruct((chunks,) + square, BF16)] * 2,
        in_specs=[vmem],
        out_specs=[vmem] * 2,
        scratch_shapes=[pltpu.VMEM((2,) + square, F32)],
        compiler_params=params,
        cost_estimate=pl.CostEstimate(flops=2**20, bytes_accessed=2**10, transcendentals=0),
        name="src_operator",
    )(found)
    if n_src == 4:
        at, slot = lax.axis_index("src"), lax.axis_index("freq")
        from_one = jnp.where(up, one[0, edge - 1 :], one[0, :1])
        other = jnp.logical_or(jnp.logical_and(at == 1, slot == 1), jnp.logical_and(at == 2, slot == 1))
        from_far = jnp.where(jnp.logical_or(other, slot > 1), 0.0, far)
        near, src_high = lax.optimization_barrier((from_one + from_far, src_high))
        if n_freq == 2:
            images = [image, near, lax.ppermute(near, "freq", [(0, 1), (1, 0)])]
        else:
            images = [image, lax.psum(near, "freq")]
    else:
        images = [lax.psum(image, "src")]
    sunk, parts = pl.pallas_call(
        inner_kernel,
        out_shape=[jax.ShapeDtypeStruct((2, rows, width), F32), jax.ShapeDtypeStruct((chunks,) + square, F32)],
        in_specs=[vmem] * 4,
        out_specs=[vmem] * 2,
        compiler_params=params,
        cost_estimate=cost,
        name="inner",
    )(field, one, src_high, src_low)
    span = -(-edge // 16) * 16
    anywhere = pl.BlockSpec(memory_space=pl.ANY)
    sunk, image = pl.pallas_call(
        source_kernel,
        out_shape=[jax.ShapeDtypeStruct((2, rows, width), F32), jax.ShapeDtypeStruct((1, width), F32)],
        in_specs=[anywhere] + [vmem] * (4 + len(images)),
        out_specs=[anywhere] * 2,
        scratch_shapes=[
            pltpu.VMEM((2, span, width), F32),
            pltpu.VMEM((1, width), F32),
            pltpu.SemaphoreType.DMA((2,)),
        ],
        input_output_aliases={0: 0},
        compiler_params=params,
        name="sources",
    )(sunk, parts, two, src_high, src_low, *images)
    return sunk.reshape(wavefield.shape), image.reshape(width)


def solution(mesh):
    in_specs = (P(None, "freq", "src", "rcv"), P(), P(), P(), P(), P("freq"))
    out_specs = (P(None, "freq", "src", "rcv"), P("rcv"))
    return jax.shard_map(body, mesh=mesh, in_specs=in_specs, out_specs=out_specs, check_vma=False)
```

```python
import functools

import jax
import jax.numpy as jnp
from jax import lax
from jax.experimental import pallas as pl
from jax.experimental.pallas import tpu as pltpu
from jax.sharding import PartitionSpec as P

SUBSTEPS = 4
TILE = 16
VMEM_LIMIT = 32 * 1024 * 1024
F32 = jnp.float32
BF16 = jnp.bfloat16


def halves(value):
    high = value.astype(BF16)
    low = (value - high.astype(F32)).astype(BF16)
    return high, low


def dot(left, right):
    return jnp.dot(left, right, preferred_element_type=F32)


def dot3(left, right):
    left_high, left_low = left
    right_high, right_low = right
    return dot(left_high, right_high) + (dot(left_high, right_low) + dot(left_low, right_high))


def complex_product(left, right):
    first = dot3(halves(left[0]), halves(right[0]))
    second = dot3(halves(left[1]), halves(right[1]))
    third = dot3(halves(left[0] + left[1]), halves(right[0] + right[1]))
    return first - second, third - first - second


def tile_taps(lateral_tiles, starts, window, small_ref, table_ref, table):
    count = window // TILE
    slots = (small_ref.shape[0] - 2) // 2
    tiles = velocities = small_ref.shape[1]
    entries, taps = table_ref.shape[2], table_ref.shape[0]
    place = lax.broadcasted_iota(jnp.int32, (count, tiles), 0)
    place = place - jnp.where(place >= count - count // 4, count, 0)
    tile = jnp.concatenate([start // TILE + place for start in starts], axis=0)
    lane = lax.broadcasted_iota(jnp.int32, tile.shape, 1)
    velocity = jnp.sum(jnp.where(lane == tile, small_ref[:1], 0.0), axis=1, keepdims=True)
    inside = jnp.logical_and(tile[:, :1] >= 0, tile[:, :1] < lateral_tiles).astype(F32)
    chosen = lax.broadcasted_iota(jnp.int32, (slots, velocities), 0).astype(F32) == small_ref[1:2, :1]
    index = jnp.sum(jnp.where(chosen, small_ref[2 : 2 + slots], 0.0), axis=0, keepdims=True)
    weight = jnp.sum(jnp.where(chosen, small_ref[2 + slots :], 0.0), axis=0, keepdims=True)
    rows = tile.shape[0]
    hit = lax.broadcasted_iota(jnp.int32, (rows, velocities), 1).astype(F32) == velocity
    index = jnp.sum(jnp.where(hit, index, 0.0), axis=1, keepdims=True)
    weight = jnp.sum(jnp.where(hit, weight, 0.0), axis=1, keepdims=True)
    entry = lax.broadcasted_iota(jnp.int32, (rows, entries), 1).astype(F32)
    mix = jnp.where(entry == index, 1.0 - weight, 0.0) + jnp.where(entry == index + 1.0, weight, 0.0)
    mix = mix * inside
    table[...] = jnp.zeros_like(table)
    found = []
    for part in range(2):
        table[part, :taps, :] = table_ref[:, part, :]
        found.append(
            lax.dot_general(
                mix, table[part], (((1,), (1,)), ((), ())), precision=lax.Precision.HIGHEST, preferred_element_type=F32
            )
        )
    return found


def fill_band(found, first, taps, band):
    window = band.shape[1]
    for position in range(window // TILE):
        shift = (position * TILE - taps // 2) % window
        for part in range(2):
            row = found[part][first + position : first + position + 1]
            spread = jnp.broadcast_to(row, (TILE, row.shape[1]))
            slanted = pltpu.roll(spread, 0, 1, stride=1, stride_axis=0)
            wide = jnp.concatenate([slanted, jnp.zeros((TILE, window - slanted.shape[1]), F32)], axis=1)
            band[part, pl.ds(position * TILE, TILE), :] = pltpu.roll(wide, shift, 1)


def four_substeps(start, lateral, once):
    window = once[0].shape[0]
    width = window // 2
    twice = complex_product(once, once)
    four = complex_product((twice[0][:width], twice[1][:width]), twice)
    place = lax.broadcasted_iota(jnp.int32, (width, window), 1)
    cell = start + jnp.where(place < window - width // 2, place, place - window)
    inside = jnp.logical_and(cell >= 0, cell < lateral)
    return jnp.where(inside, four[0], 0.0), jnp.where(inside, four[1], 0.0)


def groups_of(rows, width, rim):
    count = width // rim
    step = -(-rows // (8 * count)) * 8
    return width // count, [(low, min(low + step, rows)) for low in range(0, rows, step)]


def pack_kernel(rim, wave_ref, one_ref, two_ref):
    rows, width = wave_ref.shape
    span, groups = groups_of(rows, width, rim)
    odd = lax.axis_index("freq") % 2 == 1
    lane = lax.broadcasted_iota(jnp.int32, one_ref.shape, 1)
    packed = []
    for sign in (1, -1):
        message = wave_ref[: groups[0][1]]
        for index, (low, high) in enumerate(groups[1:], 1):
            count = high - low
            place = lane[:count] if sign == 1 else width - 1 - lane[:count]
            moved = pltpu.roll(wave_ref[low:high], sign * index * span % width, 1)
            top = jnp.where(place // span == index, moved, message[:count])
            message = top if count == message.shape[0] else jnp.concatenate([top, message[count:]], axis=0)
        packed.append(message)
    one_ref[...] = jnp.where(odd, packed[1], packed[0])
    two_ref[...] = jnp.where(odd, packed[0], packed[1])


def rcv_operator_kernel(
    lateral, small_ref, table_ref, full_ref, high_ref, low_ref, found_ref, table, band
):
    width = full_ref.shape[1] // 2
    taps, window = table_ref.shape[0], 2 * width
    chunks = found_ref.shape[1] * TILE // window - 1
    starts = [lax.axis_index("rcv") * width]
    starts += [(lax.axis_index("src") * chunks + chunk) * width for chunk in range(chunks)]
    found = tile_taps(lateral // TILE, starts, window, small_ref, table_ref, table)
    fill_band(found, 0, taps, band)
    for part in range(2):
        found_ref[part] = found[part]
    real, imag = four_substeps(starts[0], lateral, (band[0], band[1]))
    turned = jnp.concatenate([real.T, imag.T], axis=1)
    full_ref[...] = turned
    high_ref[...], low_ref[...] = halves(turned)


def src_operator_kernel(lateral, taps, found_ref, high_ref, low_ref, band):
    chunks, width = high_ref.shape[0], high_ref.shape[2] // 2
    found = (found_ref[0], found_ref[1])
    for chunk in range(chunks):
        start = (lax.axis_index("src") * chunks + chunk) * width
        fill_band(found, (chunk + 1) * 2 * width // TILE, taps, band)
        real, imag = four_substeps(start, lateral, (band[0], band[1]))
        high_ref[chunk], low_ref[chunk] = halves(jnp.concatenate([real, imag], axis=0))


def receiver_kernel(rim, wave_ref, first_ref, second_ref, full_ref, high_ref, low_ref, sunk_ref, one_ref, two_ref, image_ref):
    rows, width = sunk_ref.shape[1], sunk_ref.shape[2]
    half = width // 2
    span, groups = groups_of(2 * rows, width, rim)
    odd = lax.axis_index("freq") % 2 == 1
    before = jnp.where(odd, first_ref[...], second_ref[...])
    after = jnp.where(odd, second_ref[...], first_ref[...])
    halos = []
    for index, (low, high) in enumerate(groups):
        left, right = after[: high - low], before[: high - low]
        if index:
            left = pltpu.roll(left, -index * span % width, 1)
            right = pltpu.roll(right, index * span % width, 1)
        lane = lax.broadcasted_iota(jnp.int32, left.shape, 1)
        halos.append(jnp.where(lane < half, left, right))
    extended = jnp.concatenate([wave_ref[...], jnp.concatenate(halos, axis=0)], axis=1)
    full = dot3(halves(extended), (high_ref[...], low_ref[...]))
    real = full[:rows, :width] - full[rows:, width:]
    imag = full[:rows, width:] + full[rows:, :width]
    sunk_ref[0] = real
    sunk_ref[1] = imag
    chunks = rows // width
    ahead = lax.axis_index("src") * chunks - lax.axis_index("rcv")
    line = lax.broadcasted_iota(jnp.int32, (width, 2 * width), 0)
    image = jnp.zeros((1, width), F32)
    for chunk in range(chunks):
        away = ahead + chunk
        beside = jnp.logical_or(
            jnp.logical_and(away == 1, line < half), jnp.logical_and(away == -1, line >= half)
        )
        weights = jnp.where(away == 0, full_ref[:width], jnp.where(beside, full_ref[width:], 0.0))
        piece = slice(chunk * width, (chunk + 1) * width)
        terms = weights[:, :width] * real[piece] - weights[:, width:] * imag[piece]
        image = image + jnp.sum(terms, axis=0, keepdims=True)
    image_ref[...] = image
    edge = one_ref.shape[1]
    row = lax.broadcasted_iota(jnp.int32, (edge, width), 0)
    head = (jnp.where(row == edge - 1, image, real[:edge]), imag[:edge])
    tail = (jnp.where(row == 0, image, real[rows - edge :]), imag[rows - edge :])
    up = lax.axis_index("src") % 2 == 0
    for part in range(2):
        one_ref[part] = jnp.where(up, tail[part], head[part])
        two_ref[part] = jnp.where(up, head[part], tail[part])


def inner_kernel(field_ref, one_ref, high_ref, low_ref, out_ref, part_ref):
    inner = jnp.logical_and(lax.axis_index("src") > 0, lax.axis_index("src") < lax.axis_size("src") - 1)
    rows, width = field_ref.shape[1], field_ref.shape[2]
    half = width // 2
    chunks = rows // width
    up = lax.axis_index("src") % 2 == 0
    gap = jnp.zeros((half - one_ref.shape[1], width), F32)
    for chunk in range(chunks):
        low, high = chunk * width, (chunk + 1) * width
        extended = []
        for part in range(2):
            if chunk + 1 < chunks:
                after = field_ref[part, high : high + half]
            else:
                after = jnp.concatenate([jnp.where(up, one_ref[part], 0.0), gap], axis=0)
            if chunk > 0:
                before = field_ref[part, low - half : low]
            else:
                before = jnp.concatenate([gap, jnp.where(up, 0.0, one_ref[part])], axis=0)
            extended.append(jnp.concatenate([field_ref[part, low:high], after, before], axis=0))
        full = dot3((high_ref[chunk], low_ref[chunk]), halves(jnp.concatenate(extended, axis=1)))
        if chunk in (0, chunks - 1):

            @pl.when(inner)
            def _(chunk=chunk, full=full):
                part_ref[chunk] = full

        out_ref[0, low:high] = full[:width, :width] - full[width:, width:]
        out_ref[1, low:high] = full[:width, width:] + full[width:, :width]


def source_kernel(sunk_hbm, part_ref, two_ref, high_ref, low_ref, *rest):
    *image_refs, out_hbm, image_hbm, edge_ref, image_ref, sems = rest
    del sunk_hbm
    chunks, width = part_ref.shape[0], two_ref.shape[2]
    half, edge, span = width // 2, two_ref.shape[1], edge_ref.shape[1]
    at = lax.axis_index("src")
    up = at % 2 == 0
    inner = jnp.logical_and(at > 0, at < lax.axis_size("src") - 1)
    image = functools.reduce(jnp.add, [ref[...] for ref in image_refs])
    if len(image_refs) > 1:
        from_two = jnp.where(up, two_ref[0, :1], two_ref[0, edge - 1 :])
        image = image + jnp.where(inner, from_two, 0.0)
    image_ref[...] = image
    image_copy = pltpu.make_async_copy(image_ref, image_hbm, sems.at[0])
    image_copy.start()

    @pl.when(inner)
    def _():
        none = jnp.zeros((half, width), F32)
        gap = none[: half - edge]
        first, last = slice(0, span), slice(width - span, width)

        def pick(ref, columns):
            chosen = [
                jnp.concatenate([ref[chunk, :width, columns][rows], ref[chunk, width:, columns][rows]], axis=0)
                for chunk, rows in ((0, first), (chunks - 1, last))
            ]
            return jnp.where(up, *chosen)

        halo = []
        for part in range(2):
            before = jnp.concatenate([none, gap, two_ref[part]], axis=0)
            after = jnp.concatenate([two_ref[part], gap, none], axis=0)
            halo.append(jnp.where(up, before, after))
        beside = slice(width, 2 * width)
        operator = (pick(high_ref, beside), pick(low_ref, beside))
        full = pick(part_ref, slice(None)) + dot3(operator, halves(jnp.concatenate(halo, axis=1)))
        edge_ref[0] = full[:span, :width] - full[span:, width:]
        edge_ref[1] = full[:span, width:] + full[span:, :width]
        rows = pl.ds(pl.multiple_of(jnp.where(up, 0, chunks * width - span), 8), span)
        copy = pltpu.make_async_copy(edge_ref, out_hbm.at[:, rows, :], sems.at[1])
        copy.start()
        copy.wait()

    image_copy.wait()


def around(rcv, freq, sign):
    pairs = []
    for at in range(rcv):
        for slot in range(freq):
            target = at + (sign if slot % 2 == 0 else -sign)
            to_slot = slot
            if not 0 <= target < rcv:
                target, to_slot = at, slot ^ 1
            pairs.append((at * freq + slot, target * freq + to_slot))
    return pairs


def between(src, freq):
    pairs = []
    for at in range(src):
        target = at - 1 if at % 2 == 0 else at + 1
        for slot in range(freq):
            ends = not 0 <= target < src
            pairs.append((at * freq + slot, at * freq + (slot ^ 1) if ends else target * freq + slot))
    return pairs


def far_pairs(freq):
    pairs = []
    for slot in range(0, freq, 2):
        moves = {(1, 0): (1, 1), (2, 0): (2, 1), (0, 0): (3, 1), (3, 1): (0, 1), (0, 1): (2, 0), (2, 1): (0, 0), (3, 0): (1, 0), (1, 1): (3, 0)}
        for (at, side), (to, to_side) in sorted(moves.items()):
            pairs.append((at * freq + slot + side, to * freq + slot + to_side))
    return pairs


def body(wavefield, op_table, vel_index, interp_index, interp_weight, freq_perm):
    rows, width = wavefield.shape[2], wavefield.shape[3]
    n_src, n_rcv, n_freq = (lax.axis_size(axis) for axis in ("src", "rcv", "freq"))
    lateral = width * n_rcv
    rim = SUBSTEPS * (op_table.shape[2] // 2)
    edge = -(-(rim + 1) // 8) * 8
    half = width // 2
    chunks = rows // width
    wave = wavefield.reshape(2 * rows, width)

    vmem = pl.BlockSpec(memory_space=pltpu.VMEM)
    anywhere = pl.BlockSpec(memory_space=pltpu.HBM)
    params = pltpu.CompilerParams(vmem_limit_bytes=VMEM_LIMIT)
    cost = pl.CostEstimate(flops=6 * 2**28, bytes_accessed=2**20, transcendentals=0)

    small = max(vel_index.shape[0], interp_index.shape[0], width)
    rows_of = lambda a: jnp.pad(a.astype(F32), ((0, 0), (0, small - a.shape[1])))
    tables = [
        jnp.concatenate(
            [rows_of(vel_index.reshape(1, -1)), jnp.pad(freq_perm, (0, small - 1)).astype(F32).reshape(1, -1), rows_of(interp_index.T), rows_of(interp_weight.T)]
        ),
        op_table.transpose(2, 0, 1),
    ]
    _, groups = groups_of(2 * rows, width, rim)
    packed = jax.ShapeDtypeStruct((groups[0][1], width), F32)
    first, second = pl.pallas_call(
        functools.partial(pack_kernel, rim),
        out_shape=[packed, packed],
        in_specs=[vmem],
        out_specs=[vmem] * 2,
        compiler_params=params,
        name="pack",
    )(wave)
    first = lax.ppermute(first, ("rcv", "freq"), around(n_rcv, n_freq, -1))
    second = lax.ppermute(second, ("rcv", "freq"), around(n_rcv, n_freq, 1))

    square = (2 * width, 2 * width)
    rcv_full, rcv_high, rcv_low, found = pl.pallas_call(
        functools.partial(rcv_operator_kernel, lateral),
        out_shape=[
            jax.ShapeDtypeStruct(square, F32),
            jax.ShapeDtypeStruct(square, BF16),
            jax.ShapeDtypeStruct(square, BF16),
            jax.ShapeDtypeStruct((2, (chunks + 1) * 2 * width // TILE, width), F32),
        ],
        in_specs=[vmem] * 2,
        out_specs=[vmem] * 4,
        scratch_shapes=[pltpu.VMEM((2, width, op_table.shape[1]), F32), pltpu.VMEM((2,) + square, F32)],
        compiler_params=params,
        cost_estimate=cost,
        name="rcv_operator",
    )(*tables)
    field, one, two, image = pl.pallas_call(
        functools.partial(receiver_kernel, rim),
        out_shape=[
            jax.ShapeDtypeStruct((2, rows, width), F32),
            jax.ShapeDtypeStruct((2, edge, width), F32),
            jax.ShapeDtypeStruct((2, edge, width), F32),
            jax.ShapeDtypeStruct((1, width), F32),
        ],
        in_specs=[vmem] * 6,
        out_specs=[vmem] * 4,
        compiler_params=params,
        name="receivers",
    )(wave, first, second, rcv_full, rcv_high, rcv_low)

    if n_freq == 2:
        other = lax.ppermute(one, "freq", [(0, 1), (1, 0)])
        image = image + jnp.where(lax.axis_index("src") % 2 == 0, other[0, :1], other[0, edge - 1 :])
    else:
        image = lax.psum(image, "freq")
    one = lax.ppermute(one, "src", [(i, i + 1 if i % 2 == 0 else i - 1) for i in range(n_src)])
    up = lax.axis_index("src") % 2 == 0
    if n_src == 4:
        far = lax.ppermute(image, ("src", "freq"), far_pairs(n_freq))
        two = lax.dynamic_update_slice(two, image[None], (0, jnp.where(up, edge - 1, 0), 0))
    two, found = lax.optimization_barrier((two, found))
    two = lax.ppermute(two, ("src", "freq"), between(n_src, n_freq))
    src_high, src_low = pl.pallas_call(
        functools.partial(src_operator_kernel, lateral, op_table.shape[2]),
        out_shape=[jax.ShapeDtypeStruct((chunks,) + square, BF16)] * 2,
        in_specs=[vmem],
        out_specs=[vmem] * 2,
        scratch_shapes=[pltpu.VMEM((2,) + square, F32)],
        compiler_params=params,
        cost_estimate=pl.CostEstimate(flops=2**20, bytes_accessed=2**10, transcendentals=0),
        name="src_operator",
    )(found)
    if n_src == 4:
        at, slot = lax.axis_index("src"), lax.axis_index("freq")
        from_one = jnp.where(up, one[0, edge - 1 :], one[0, :1])
        other = jnp.logical_or(jnp.logical_and(at == 1, slot == 1), jnp.logical_and(at == 2, slot == 1))
        from_far = jnp.where(jnp.logical_or(other, slot > 1), 0.0, far)
        near, src_high = lax.optimization_barrier((from_one + from_far, src_high))
        if n_freq == 2:
            images = [image, near, lax.ppermute(near, "freq", [(0, 1), (1, 0)])]
        else:
            images = [image, lax.psum(near, "freq")]
    else:
        images = [lax.psum(image, "src")]
    sunk, parts = pl.pallas_call(
        inner_kernel,
        out_shape=[jax.ShapeDtypeStruct((2, rows, width), F32), jax.ShapeDtypeStruct((chunks,) + square, F32)],
        in_specs=[vmem] * 4,
        out_specs=[vmem] * 2,
        compiler_params=params,
        cost_estimate=cost,
        name="inner",
    )(field, one, src_high, src_low)
    span = -(-edge // 16) * 16
    anywhere = pl.BlockSpec(memory_space=pl.ANY)
    sunk, image = pl.pallas_call(
        source_kernel,
        out_shape=[jax.ShapeDtypeStruct((2, rows, width), F32), jax.ShapeDtypeStruct((1, width), F32)],
        in_specs=[anywhere] + [vmem] * (4 + len(images)),
        out_specs=[anywhere] * 2,
        scratch_shapes=[
            pltpu.VMEM((2, span, width), F32),
            pltpu.VMEM((1, width), F32),
            pltpu.SemaphoreType.DMA((2,)),
        ],
        input_output_aliases={0: 0},
        compiler_params=params,
        name="sources",
    )(sunk, parts, two, src_high, src_low, *images)
    return sunk.reshape(wavefield.shape), image.reshape(width)


def solution(mesh):
    in_specs = (P(None, "freq", "src", "rcv"), P(), P(), P(), P(), P("freq"))
    out_specs = (P(None, "freq", "src", "rcv"), P("rcv"))
    return jax.shard_map(body, mesh=mesh, in_specs=in_specs, out_specs=out_specs, check_vma=False)
```
